512 devices in a mesh: tile: 128 (over z, y, core), sub: 4 (over x).
Axes of the slice: x: 4, y: 8, z: 8, core: 2. Of those that a mesh axis runs over, the one named last changes fastest.
Arguments:
- right_side: float32 [10, 16, 512, 512], P(None, None, 'tile', 'sub'), may hold values from -24 to 24
- fine_coeffs: float32 [5, 10, 10, 512, 512], P(None, None, None, 'tile', 'sub')
- fine_inverse: float32 [10, 10, 512, 512], P(None, None, 'tile', 'sub')
- aggregate: int32 [512, 512], P('tile', 'sub'), may hold values from 0 to 63, as said below
- coarse_coeffs: float32 [5, 10, 10, 32768], P(None, None, None, 'tile')
- coarse_inverse: float32 [10, 10, 32768], P(None, None, 'tile')
- coarse_cols: int32 [5, 32768], P(None, 'tile'), may hold values from 0 to 319, as said below
- send_rows: int32 [2, 4096], P(None, 'tile'), may hold values from 0 to 207, as said below
Outputs:
- solution: float32 [10, 16, 512, 512], P(None, None, 'tile', 'sub')
The draws below stay inside these ranges and needn't reach their ends.
Inputs may be any that keep to these rules, and one draw needn't show every extreme that they name: On each device the aggregate numbers in use are 0 to n - 1, each held by one or more cells, with n = 64 on the devices of sub index 0, 32 at index 1 and 16 at higher indices. `coarse_cols`: entry 0 of every row is the row itself within its group. Rows that no cell maps to name only themselves, and no other row names them; the other entries name such live rows of the group (below 256) or received rows (256 and above). `send_rows`: every entry is a live row of its group, as numbered within the group, a row that some cell maps to.
All inputs are finite; a program needn't handle non-finite values.
Results may differ from the reference program's by a relative error of at most 0.00007.
Values sent between devices are 32-bit elements; how exact they have to be, the bound alone decides.
No kernel may reach another device: no remote copies, remote signals or barrier semaphores. Data moves between devices by JAX's collectives and lax.ppermute only.
A program may use at most 128 MiB of HBM per device.

```python
import jax
import jax.numpy as jnp
from jax import lax

FIELDS = 10
COLS = 16
CX = 4
CY = 128
KC = 5
CSWEEP = 4
CAPC = 64
HALOC = 32
ROWSG = 256
COARSE = 32768
NX = 512
NY = 512


def cell_gain(key, shape):
    return jnp.exp(jax.random.uniform(key, shape, jnp.float32, -0.69, 0.69))


def identity_mask(shape, row_dim, col_dim):
    row_axis = lax.broadcasted_iota(jnp.int32, shape, row_dim)
    col_axis = lax.broadcasted_iota(jnp.int32, shape, col_dim)
    return (row_axis == col_axis).astype(jnp.float32)


def live_counts(sub_count):
    return [CAPC * (4 >> min(position, 2)) // 4 for position in range(sub_count)]


def rank_to_row(rank, counts):
    row_number = rank
    boundary = 0
    for position in range(1, len(counts)):
        boundary = boundary + counts[position - 1]
        row_number = row_number + (CAPC - counts[position - 1]) * (rank >= boundary).astype(jnp.int32)
    return row_number


def draw_fine_coeffs(key, part):
    gains = cell_gain(jax.random.fold_in(key, 101), (NX, NY))
    key = jax.random.fold_in(key, 1)
    jitter = 0.1 * jax.random.normal(key, (5, FIELDS, FIELDS, NX, NY), jnp.float32)
    term_axis = lax.broadcasted_iota(jnp.int32, (5, FIELDS, FIELDS, 1, 1), 0)
    centre = 4.0 * identity_mask((5, FIELDS, FIELDS, 1, 1), 1, 2) * (term_axis == 0).astype(jnp.float32)
    return (centre + jitter) * gains[None, None, None]


def draw_fine_inverse(key, part):
    gains = cell_gain(jax.random.fold_in(key, 101), (NX, NY))
    key = jax.random.fold_in(key, 2)
    jitter = 0.05 * jax.random.normal(key, (FIELDS, FIELDS, NX, NY), jnp.float32)
    return (identity_mask((FIELDS, FIELDS, 1, 1), 0, 1) + jitter) / (4.0 * gains[None, None])


def draw_coarse_coeffs(key, part):
    gains = cell_gain(jax.random.fold_in(key, 102), (COARSE,))
    key = jax.random.fold_in(key, 3)
    jitter = 0.15 * jax.random.normal(key, (KC, FIELDS, FIELDS, COARSE), jnp.float32)
    term_axis = lax.broadcasted_iota(jnp.int32, (KC, FIELDS, FIELDS, 1), 0)
    centre = 6.0 * identity_mask((KC, FIELDS, FIELDS, 1), 1, 2) * (term_axis == 0).astype(jnp.float32)
    return (centre + jitter) * gains[None, None, None]


def draw_coarse_inverse(key, part):
    gains = cell_gain(jax.random.fold_in(key, 102), (COARSE,))
    key = jax.random.fold_in(key, 4)
    jitter = 0.05 * jax.random.normal(key, (FIELDS, FIELDS, COARSE), jnp.float32)
    return (identity_mask((FIELDS, FIELDS, 1), 0, 1) + jitter) / (6.0 * gains[None, None])


def draw_aggregate(key, part):
    key = jax.random.fold_in(key, 11)
    tile_count = NX // CX
    sub_count = NY // CY
    band_count = CAPC // 4
    scores = jax.random.randint(key, (tile_count, sub_count, CY - 1), 0, 1 << 20)
    scores = scores * CY + jnp.arange(CY - 1, dtype=jnp.int32)
    cut_points = lax.top_k(scores, band_count - 1)[1].astype(jnp.int32) + 1
    position = jnp.arange(CY, dtype=jnp.int32)
    band = jnp.sum((cut_points[:, :, None, :] <= position[None, None, :, None]).astype(jnp.int32), axis=-1)
    sub_number = jnp.arange(sub_count, dtype=jnp.int32)
    strips = jnp.where(sub_number == 0, 4, jnp.where(sub_number == 1, 2, 1))
    strip = jnp.arange(CX, dtype=jnp.int32)[None, :] * strips[:, None] // CX
    labels = strip[None, :, :, None] * band_count + band[:, :, None, :]
    return labels.transpose(0, 2, 1, 3).reshape(NX, NY).astype(jnp.int32)


def draw_coarse_cols(key, part):
    key = jax.random.fold_in(key, 12)
    sub_count = ROWSG // CAPC
    counts = live_counts(sub_count)
    live_total = sum(counts)
    picks = jax.random.randint(key, (KC - 1, COARSE), 0, live_total + 2 * HALOC)
    inside = rank_to_row(picks, counts)
    chosen = jnp.where(picks < live_total, inside, ROWSG + picks - live_total)
    local_row = jnp.arange(COARSE, dtype=jnp.int32) % ROWSG
    owner = local_row // CAPC
    live_limit = jnp.zeros_like(local_row)
    for position in range(sub_count):
        live_limit = live_limit + counts[position] * (owner == position).astype(jnp.int32)
    padding = local_row % CAPC >= live_limit
    chosen = jnp.where(padding[None], local_row[None], chosen)
    chosen = chosen.at[0, 0].set(ROWSG + 2 * HALOC - 1)
    return jnp.concatenate([local_row[None], chosen], axis=0).astype(jnp.int32)


def draw_send_rows(key, part):
    key = jax.random.fold_in(key, 13)
    sub_count = ROWSG // CAPC
    group_count = COARSE // ROWSG
    counts = live_counts(sub_count)
    live_total = sum(counts)
    scores = jax.random.randint(key, (2, group_count, live_total), 0, 1 << 20)
    scores = scores * live_total + jnp.arange(live_total, dtype=jnp.int32)
    ranks = lax.top_k(scores, HALOC)[1].astype(jnp.int32)
    rows_sent = rank_to_row(ranks, counts)
    rows_sent = rows_sent.at[0, 0, 0].set(rank_to_row(jnp.int32(live_total - 1), counts))
    rows_sent = rows_sent.at[1, 0, 0].set(0)
    return rows_sent.reshape(2, group_count * HALOC).astype(jnp.int32)


def shard_levels(stream_key, dims, split, least, top_value):
    def one(axis_at, shards_of):
        heights = jax.random.uniform(jax.random.fold_in(jax.random.fold_in(stream_key, 6), axis_at), (shards_of,), jnp.float32, least / len(split), top_value / len(split))
        return jnp.repeat(jnp.exp(heights), dims[axis_at] // shards_of).reshape((-1,) + (1,) * (len(dims) - axis_at - 1))

    factor_of = one(*split[0])
    for cut in split[1:]:
        factor_of = factor_of * one(*cut)
    return factor_of


def centred(key, dims, deviation, limit, split=(), kind=jnp.bfloat16):
    gain = shard_levels(key, dims, split, -0.22, 0.18) if split else 1.0
    array = jax.random.normal(key, dims, jnp.float32) * deviation * gain
    return jnp.minimum(jnp.maximum(array, -limit), limit).astype(kind)


def setup_inputs(seed: int = 0) -> dict:
    key_list = jax.random.split(jax.random.key(seed), 9)
    right_side = centred(key_list[0], (FIELDS, COLS, NX, NY), 4.0, 24.0, ((2, 128), (3, 4)), jnp.float32)
    fine_coeffs = draw_fine_coeffs(jax.random.fold_in(key_list[8], 71), 0)
    fine_inverse = draw_fine_inverse(jax.random.fold_in(key_list[8], 71), 0)
    aggregate = draw_aggregate(jax.random.fold_in(key_list[8], 71), 0)
    coarse_coeffs = draw_coarse_coeffs(jax.random.fold_in(key_list[8], 71), 0)
    coarse_inverse = draw_coarse_inverse(jax.random.fold_in(key_list[8], 71), 0)
    coarse_cols = draw_coarse_cols(jax.random.fold_in(key_list[8], 71), 0)
    send_rows = draw_send_rows(jax.random.fold_in(key_list[8], 71), 0)
    return dict(right_side=right_side, fine_coeffs=fine_coeffs, fine_inverse=fine_inverse, aggregate=aggregate, coarse_coeffs=coarse_coeffs, coarse_inverse=coarse_inverse, coarse_cols=coarse_cols, send_rows=send_rows)


OMEGA = 0.7
THETA = 0.6


def block_apply(coeffs, vector):
    summed = coeffs[:, 0][:, None] * vector[0][None]
    for source in range(1, coeffs.shape[1]):
        summed = summed + coeffs[:, source][:, None] * vector[source][None]
    return summed


def fine_operator(coeffs, vector):
    padded = jnp.pad(vector, ((0, 0), (0, 0), (1, 1), (1, 1)))
    result = block_apply(coeffs[0], vector)
    result = result + block_apply(coeffs[1], padded[:, :, :-2, 1:-1])
    result = result + block_apply(coeffs[2], padded[:, :, 2:, 1:-1])
    result = result + block_apply(coeffs[3], padded[:, :, 1:-1, :-2])
    result = result + block_apply(coeffs[4], padded[:, :, 1:-1, 2:])
    return result


def coarse_operator(coeffs, coarse_cols, send_rows, vector):
    fields, columns, count = vector.shape
    groups = count // ROWSG
    grouped = vector.reshape(fields, columns, groups, ROWSG)
    send_lists = send_rows.reshape(2, groups, HALOC)

    def pick_rows(row_table):
        wide_table = jnp.broadcast_to(row_table[None, None], (fields, columns) + row_table.shape)
        return jnp.take_along_axis(grouped, wide_table, axis=3)

    to_left = pick_rows(send_lists[0])
    to_right = pick_rows(send_lists[1])
    blank_rows = jnp.zeros((fields, columns, 1, HALOC), vector.dtype)
    from_left = jnp.concatenate([blank_rows, to_right[:, :, :-1]], axis=2)
    from_right = jnp.concatenate([to_left[:, :, 1:], blank_rows], axis=2)
    extended = jnp.concatenate([grouped, from_left, from_right], axis=3)
    col_table = coarse_cols.reshape(coarse_cols.shape[0], groups, ROWSG)
    result = jnp.zeros_like(grouped)
    for term_index in range(coeffs.shape[0]):
        wide_table = jnp.broadcast_to(col_table[term_index][None, None], (fields, columns, groups, ROWSG))
        gathered = jnp.take_along_axis(extended, wide_table, axis=3)
        result = result + block_apply(coeffs[term_index].reshape(fields, fields, groups, ROWSG), gathered)
    return result.reshape(fields, columns, count)


def reference(right_side, fine_coeffs, fine_inverse, aggregate, coarse_coeffs, coarse_inverse, coarse_cols, send_rows):
    fields, columns, first_extent, second_extent = right_side.shape

    def smooth(vector):
        return vector + OMEGA * block_apply(fine_inverse, right_side - fine_operator(fine_coeffs, vector))

    smoothed = smooth(OMEGA * block_apply(fine_inverse, right_side))
    residual = right_side - fine_operator(fine_coeffs, smoothed)
    filtered = residual - THETA * fine_operator(fine_coeffs, block_apply(fine_inverse, residual))
    first_group = jnp.arange(first_extent, dtype=jnp.int32) // CX
    second_group = jnp.arange(second_extent, dtype=jnp.int32) // CY
    coarse_index = first_group[:, None] * ROWSG + second_group[None, :] * CAPC + aggregate
    flat_index = coarse_index.reshape(-1).astype(jnp.int32)
    coarse_rhs = jax.ops.segment_sum(filtered.reshape(fields * columns, -1).T, flat_index, num_segments=COARSE)
    coarse_rhs = coarse_rhs.T.reshape(fields, columns, COARSE)
    coarse_level = OMEGA * block_apply(coarse_inverse, coarse_rhs)
    for sweep_index in range(CSWEEP - 1):
        coarse_level = coarse_level + OMEGA * block_apply(
            coarse_inverse, coarse_rhs - coarse_operator(coarse_coeffs, coarse_cols, send_rows, coarse_level))
    spread = jnp.take(coarse_level.reshape(fields * columns, COARSE), flat_index, axis=1).reshape(right_side.shape)
    correction = spread - THETA * block_apply(fine_inverse, fine_operator(fine_coeffs, spread))
    solution = smooth(smoothed + correction)
    return solution
```

```python
import jax
import jax.numpy as jnp
from jax import lax
from jax.experimental import pallas as pl
from jax.experimental.pallas import tpu as pltpu
from jax.sharding import PartitionSpec as P

CSWEEP = 4
OMEGA = 0.7
THETA = 0.6
FC = 160
SLABS = 5
NIJ = 504
IJ = 104
EDGE = 176
F32 = jnp.float32
I32 = jnp.int32

VM = pl.BlockSpec(memory_space=pltpu.VMEM)
SM = pl.BlockSpec(memory_space=pltpu.SMEM)


def lanes():
    return lax.broadcasted_iota(I32, (8, 128), 1)


def roll(value, shift):
    shift = shift % 128
    return pltpu.roll(value, shift, 1) if shift else value


def pick(value, index):
    return jnp.take_along_axis(value, index, axis=1, mode="promise_in_bounds")


def row(ref, at):
    return jnp.broadcast_to(ref[pl.ds(at, 1), :], (8, 128))


def call(kernel, outs, args, scratch=(), flops=1000000):
    specs = [SM] + [VM] * (len(args) - 1)
    return pl.pallas_call(
        kernel,
        out_shape=[jax.ShapeDtypeStruct(s, F32) for s in outs],
        in_specs=specs,
        out_specs=[VM] * len(outs),
        scratch_shapes=[pltpu.VMEM(s, F32) for s in scratch],
        compiler_params=pltpu.CompilerParams(vmem_limit_bytes=24 * 1024 * 1024),
    )(*args)


def strip_groups():
    groups = []
    for start in range(0, FC, 8):
        groups.append(("r", start))
    for start in list(range(0, 96, 8)) + [92]:
        groups.append(("j", start))
    for start in list(range(0, 496, 8)) + [492]:
        groups.append(("a", start))
    groups.append(("g", 0))
    return groups


GROUPS = strip_groups()
PACKED = (len(GROUPS) + 3) // 4 * 8


def slot_columns(lane):
    slot = lane & 7
    column = jnp.where(slot <= 2, 2 - slot, jnp.where(slot >= 5, 132 - slot, jnp.where(slot == 3, 127, 0)))
    return column


def pack_kernel(meta, rhs, inverse, coeffs, aggregate, out):
    lane = lanes()
    index = slot_columns(lane)
    window = lane >> 3
    sources = {"r": rhs, "j": inverse, "a": coeffs}
    for q in range(PACKED // 8):
        packed = jnp.zeros((8, 128), F32)
        for k, (kind, start) in enumerate(GROUPS[4 * q : 4 * q + 4]):
            for x in range(4):
                if kind == "g":
                    block = jnp.broadcast_to(aggregate[pl.ds(x, 1), :].astype(F32), (8, 128))
                else:
                    block = sources[kind][pl.ds(4 * start + x, 8, stride=4), :]
                packed = jnp.where(window == 4 * k + x, pick(block, index), packed)
        out[pl.ds(8 * q, 8), :] = packed


def block_rows(coeff_row, vectors):
    out = []
    for i in range(10):
        pair = None
        for j in range(10):
            m = coeff_row(i, j)
            if pair is None:
                pair = [m * vectors[2 * j], m * vectors[2 * j + 1]]
            else:
                pair = [pair[0] + m * vectors[2 * j], pair[1] + m * vectors[2 * j + 1]]
        out += pair
    return out


def load_slab(ref, base):
    return [ref[pl.ds(base + 8 * b, 8), :] for b in range(20)]


def store_slab(ref, base, values):
    for b in range(20):
        ref[pl.ds(base + 8 * b, 8), :] = values[b]


def inverse_at(inverse, x, vectors):
    base = pl.multiple_of(x * IJ, 8)
    return block_rows(lambda i, j: row(inverse, base + (10 * i + j)), vectors)


def stencil_at(coeffs, shifted, x):
    total = None
    for n in range(5):
        vectors = load_slab(shifted, pl.multiple_of((n * SLABS + x) * FC, 8))
        base = pl.multiple_of(x * NIJ, 4) + 100 * n
        part = block_rows(lambda i, j: row(coeffs, base + (10 * i + j)), vectors)
        total = part if total is None else [a + b for a, b in zip(total, part)]
    return total


def write_edges(meta, vector, edge_a, edge_b):
    lane = lanes()
    odd = meta[0]
    for out, x in ((edge_a, 3 * (1 - odd)), (edge_b, 3 * odd)):
        base = pl.multiple_of(x * FC, 8)
        for b in range(20):
            out[pl.ds(8 * b, 8), :] = vector[pl.ds(base + 8 * b, 8), :]
        for h in range(2):
            packed = jnp.zeros((8, 128), F32)
            for f in range(10):
                strip = vector[pl.ds(4 * FC + 16 * f + 8 * h, 8), :]
                moved = pltpu.roll(strip, lax.rem(8 * f + 120 - 8 * x, 128), 1)
                packed = jnp.where((lane >> 3) == f, moved, packed)
            out[pl.ds(FC + 8 * h, 8), :] = packed


def shift_all(meta, vector, got_a, got_b, shifted):
    lane = lanes()
    odd = meta[0] == 1
    slot = lane & 7
    window = lane >> 3

    def put(n, x, b, value):
        shifted[pl.ds((n * SLABS + x) * FC + 8 * b, 8), :] = value

    strips = []
    for h in range(2):
        a, b = got_a[pl.ds(FC + 8 * h, 8), :], got_b[pl.ds(FC + 8 * h, 8), :]
        strips.append((jnp.where(odd, a, b), jnp.where(odd, b, a)))
    for b in range(20):
        f, h = b // 2, b % 2
        a_row, b_row = got_a[pl.ds(8 * b, 8), :], got_b[pl.ds(8 * b, 8), :]
        before, after = jnp.where(odd, a_row, b_row), jnp.where(odd, b_row, a_row)
        main = [vector[pl.ds(x * FC + 8 * b, 8), :] for x in range(4)]
        strip = vector[pl.ds(4 * FC + 8 * b, 8), :]
        strip = jnp.where(window == 0, roll(strips[h][0], -8 * f), strip)
        strip = jnp.where(window == 5, roll(strips[h][1], 40 - 8 * f), strip)
        for x in range(4):
            own = (window == x + 1) & ((slot == 3) | (slot == 4))
            strip = jnp.where(own, roll(main[x], 8 * (x + 1) + 4), strip)
        wall = [before] + main + [after]
        for x in range(4):
            put(0, x, b, main[x])
            put(1, x, b, wall[x])
            put(2, x, b, wall[x + 2])
            put(3, x, b, jnp.where(lane == 0, roll(strip, -(8 * (x + 1) + 5)), roll(main[x], 1)))
            put(4, x, b, jnp.where(lane == 127, roll(strip, 127 - (8 * (x + 1) + 2)), roll(main[x], -1)))
        put(0, 4, b, strip)
        put(1, 4, b, roll(strip, 8))
        put(2, 4, b, roll(strip, -8))
        put(3, 4, b, roll(strip, -1))
        put(4, 4, b, roll(strip, 1))


def first_kernel(meta, rhs, inverse, coeffs, got_1, got_2, coeffs_x, inverse_x, rhs_x, index_s, first, edge_a, edge_b):
    lane = lanes()
    slot = lane & 7
    window = lane >> 3
    odd = lax.rem(meta[1], 2) == 1
    inside = (window >= 1) & (window <= 4)
    needed = inside & ((slot == 1) | (slot == 2) | (slot == 5) | (slot == 6))
    for q in range(PACKED // 8):
        one, two = got_1[pl.ds(8 * q, 8), :], got_2[pl.ds(8 * q, 8), :]
        left, right = jnp.where(odd, one, two), jnp.where(odd, two, one)
        both = jnp.where(slot <= 2, right, jnp.where(slot >= 5, left, 0.0))
        for k, (kind, start) in enumerate(GROUPS[4 * q : 4 * q + 4]):
            placed = roll(both, 8 - 32 * k)
            if kind == "r":
                rhs_x[pl.ds(4 * FC + start, 8), :] = jnp.where(inside, placed, 0.0)
            elif kind == "j":
                inverse_x[pl.ds(4 * IJ + start, 8), :] = jnp.where(inside, placed, 0.0)
            elif kind == "a":
                coeffs_x[pl.ds(4 * NIJ + start, 8), :] = jnp.where(needed, placed, 0.0)
            else:
                index_s[...] = jnp.where(inside, placed, 0.0)
    for x in range(4):
        for kind, start in GROUPS:
            if kind == "r":
                rhs_x[pl.ds(x * FC + start, 8), :] = rhs[pl.ds(4 * start + x, 8, stride=4), :]
            elif kind == "j":
                inverse_x[pl.ds(x * IJ + start, 8), :] = inverse[pl.ds(4 * start + x, 8, stride=4), :]
            elif kind == "a":
                coeffs_x[pl.ds(x * NIJ + start, 8), :] = coeffs[pl.ds(4 * start + x, 8, stride=4), :]

    def at(x, carry):
        base = pl.multiple_of(x * FC, 8)
        values = inverse_at(inverse_x, x, load_slab(rhs_x, base))
        store_slab(first, base, [OMEGA * v for v in values])
        return carry

    lax.fori_loop(0, SLABS, at, 0)
    write_edges(meta, first, edge_a, edge_b)


def smooth_kernel(meta, coeffs_x, inverse_x, rhs_x, first, got_a, got_b, smoothed, edge_a, edge_b, shifted):
    shift_all(meta, first, got_a, got_b, shifted)

    def at(x, carry):
        base = pl.multiple_of(x * FC, 8)
        total = stencil_at(coeffs_x, shifted, x)
        left = [r - t for r, t in zip(load_slab(rhs_x, base), total)]
        step = inverse_at(inverse_x, x, left)
        store_slab(smoothed, base, [v + OMEGA * s for v, s in zip(load_slab(first, base), step)])
        return carry

    lax.fori_loop(0, SLABS, at, 0)
    write_edges(meta, smoothed, edge_a, edge_b)


def residual_kernel(meta, coeffs_x, inverse_x, rhs_x, smoothed, got_a, got_b, residual, scaled, edge_a, edge_b, shifted):
    shift_all(meta, smoothed, got_a, got_b, shifted)

    def at(x, carry):
        base = pl.multiple_of(x * FC, 8)
        total = stencil_at(coeffs_x, shifted, x)
        left = [r - t for r, t in zip(load_slab(rhs_x, base), total)]
        store_slab(residual, base, left)
        store_slab(scaled, base, inverse_at(inverse_x, x, left))
        return carry

    lax.fori_loop(0, SLABS, at, 0)
    write_edges(meta, scaled, edge_a, edge_b)


def gather_kernel(meta, coeffs_x, residual, scaled, aggregate, got_a, got_b, out, shifted, filtered):
    shift_all(meta, scaled, got_a, got_b, shifted)

    def at(x, carry):
        base = pl.multiple_of(x * FC, 8)
        total = stencil_at(coeffs_x, shifted, x)
        store_slab(filtered, base, [r - THETA * t for r, t in zip(load_slab(residual, base), total)])
        return carry

    lax.fori_loop(0, 4, at, 0)
    member = lax.broadcasted_iota(I32, (128, 128), 0) & 63
    summed = jnp.zeros((FC, 128), F32)
    for x in range(4):
        owner = jnp.broadcast_to(aggregate[pl.ds(x, 1), :], (128, 128))
        table = (owner == member).astype(jnp.float32).astype(jnp.bfloat16)
        rest = filtered[pl.ds(x * FC, FC), :]
        for _ in range(3):
            part = rest.astype(jnp.bfloat16)
            rest = rest - part.astype(F32)
            summed = summed + lax.dot_general(
                part, table, (((1,), (1,)), ((), ())), preferred_element_type=F32
            )
    low = lax.broadcasted_iota(I32, (80, 128), 1) < 64
    packed = jnp.where(low, summed[:80], summed[80:])
    for s in range(4):
        out[s] = packed


def live_lane(index):
    lane = jnp.where(index < 96, index, jnp.where(index < 192, index - 32, index - 80))
    return jnp.where(index >= 256, index - 128, lane)


def live(low, high, lane):
    return jnp.where(lane < 96, low, jnp.where(lane < 112, roll(high, 96), roll(high, 48)))


def send_coarse(meta, index, level, out_a, out_b):
    lane = lanes()
    odd = meta[0] == 1
    tables = []
    for d in range(2):
        four = jnp.concatenate([index[pl.ds(d, 1), :]] * 4, axis=1)
        tables.append(jnp.broadcast_to(live_lane(four), (8, 128)))
    for out, table in (
        (out_a, jnp.where(odd, tables[0], tables[1])),
        (out_b, jnp.where(odd, tables[1], tables[0])),
    ):
        for g in range(5):
            packed = jnp.zeros((8, 128), F32)
            for k in range(4):
                value = pick(level[pl.ds(8 * (4 * g + k), 8), :], table)
                packed = jnp.where((lane >> 5) == k, value, packed)
            out[pl.ds(8 * g, 8), :] = packed


def coarse_start_kernel(meta, got, coeffs, inverse, send, rhs, level, coeffs_l, inverse_l, out_a, out_b):
    lane = lanes()
    for b in range(20):
        r = 8 * (b % 10)
        up = 64 * (b // 10)
        part = [got[s, pl.ds(r, 8), :] for s in range(4)]
        value = jnp.where(lane < 64, roll(part[0], -up), roll(part[1], 64 - up))
        value = jnp.where(lane < 96, value, jnp.where(lane < 112, roll(part[2], 96 - up), roll(part[3], 112 - up)))
        rhs[pl.ds(8 * b, 8), :] = value
    lane10 = lax.broadcasted_iota(I32, (10, 128), 1)
    for i in range(10):
        inverse_l[i] = live(inverse[i, :, 0:128], inverse[i, :, 128:256], lane10)
    for n in range(5):
        for i in range(10):
            coeffs_l[n, i] = live(coeffs[n, i, :, 0:128], coeffs[n, i, :, 128:256], lane10)
    values = block_rows(lambda i, j: jnp.broadcast_to(inverse_l[i, pl.ds(j, 1), :], (8, 128)), load_slab(rhs, 0))
    store_slab(level, 0, [OMEGA * v for v in values])
    send_coarse(meta, send, level, out_a, out_b)


def sweep(meta, coeffs_l, inverse_l, cols, rhs, level, got_a, got_b):
    lane = lanes()
    odd = meta[0] == 1
    extra = []
    for g in range(5):
        a, b = got_a[pl.ds(8 * g, 8), :], got_b[pl.ds(8 * g, 8), :]
        before, after = jnp.where(odd, a, b), jnp.where(odd, b, a)
        for k in range(4):
            extra.append(jnp.where(lane < 32, roll(before, -32 * k), roll(after, 32 - 32 * k)))
    total = block_rows(lambda i, j: jnp.broadcast_to(coeffs_l[0, i, pl.ds(j, 1), :], (8, 128)), load_slab(level, 0))
    for n in range(1, 5):
        low, high = cols[pl.ds(n, 1), 0:128], cols[pl.ds(n, 1), 128:256]
        lane1 = lax.broadcasted_iota(I32, (8, 128), 1)
        index = live(jnp.broadcast_to(low, (8, 128)), jnp.broadcast_to(high, (8, 128)), lane1)
        index = live_lane(index)
        near = index & 127
        vectors = []
        for b in range(20):
            own = pick(level[pl.ds(8 * b, 8), :], near)
            vectors.append(jnp.where(index < 128, own, pick(extra[b], near)))
        part = block_rows(lambda i, j: jnp.broadcast_to(coeffs_l[n, i, pl.ds(j, 1), :], (8, 128)), vectors)
        total = [a + b for a, b in zip(total, part)]
    left = [r - t for r, t in zip(load_slab(rhs, 0), total)]
    step = block_rows(lambda i, j: jnp.broadcast_to(inverse_l[i, pl.ds(j, 1), :], (8, 128)), left)
    return [v + OMEGA * s for v, s in zip(load_slab(level, 0), step)]


def sweep_kernel(meta, coeffs_l, inverse_l, cols, send, rhs, level, got_a, got_b, out, out_a, out_b):
    store_slab(out, 0, sweep(meta, coeffs_l, inverse_l, cols, rhs, level, got_a, got_b))
    send_coarse(meta, send, out, out_a, out_b)


def last_sweep_kernel(
    meta, coeffs_l, inverse_l, cols, rhs, level, got_a, got_b, aggregate, index_s, spread, edge_a, edge_b
):
    lane = lanes()
    slot = lane & 7
    sub = meta[1]

    def offset(s):
        return jnp.where(s <= 0, 0, jnp.where(s == 1, 64, jnp.where(s == 2, 96, 112)))

    values = sweep(meta, coeffs_l, inverse_l, cols, rhs, level, got_a, got_b)
    for x in range(4):
        index = jnp.broadcast_to(aggregate[pl.ds(x, 1), :], (8, 128)) + offset(sub)
        store_slab(spread, x * FC, [pick(v, index) for v in values])
    index = index_s[...].astype(I32) + jnp.where(slot <= 2, offset(sub + 1), offset(sub - 1))
    window = lane >> 3
    inside = (window >= 1) & (window <= 4)
    there = inside & (((slot <= 2) & (sub < meta[2] - 1)) | ((slot >= 5) & (sub > 0)))
    index = jnp.minimum(index, 127)
    store_slab(spread, 4 * FC, [jnp.where(there, pick(v, index), 0.0) for v in values])
    write_edges(meta, spread, edge_a, edge_b)


def correct_kernel(meta, coeffs_x, inverse_x, spread, got_a, got_b, applied, scaled, edge_a, edge_b, shifted):
    shift_all(meta, spread, got_a, got_b, shifted)

    def at(x, carry):
        base = pl.multiple_of(x * FC, 8)
        total = stencil_at(coeffs_x, shifted, x)
        store_slab(applied, base, total)
        store_slab(scaled, base, inverse_at(inverse_x, x, total))
        return carry

    lax.fori_loop(0, SLABS, at, 0)
    write_edges(meta, scaled, edge_a, edge_b)


def last_kernel(
    meta, coeffs_x, inverse_x, smoothed, residual, spread, applied, scaled, got_a, got_b, out, shifted
):
    shift_all(meta, scaled, got_a, got_b, shifted)

    def at(x, carry):
        base = pl.multiple_of(x * FC, 8)
        total = stencil_at(coeffs_x, shifted, x)
        left = [
            r - a + THETA * t
            for r, a, t in zip(load_slab(residual, base), load_slab(applied, base), total)
        ]
        step = inverse_at(inverse_x, x, left)
        for b in range(20):
            at_row = pl.ds(base + 8 * b, 8)
            value = smoothed[at_row, :] + spread[at_row, :] - THETA * scaled[at_row, :] + OMEGA * step[b]
            out[pl.ds(32 * b + x, 8, stride=4), :] = value
        return carry

    lax.fori_loop(0, 4, at, 0)


def body(right_side, fine_coeffs, fine_inverse, aggregate, coarse_coeffs, coarse_inverse, coarse_cols, send_rows):
    tiles, subs = lax.axis_size("tile"), lax.axis_size("sub")
    me, sub = lax.axis_index("tile"), lax.axis_index("sub")
    meta = jnp.stack([lax.rem(me, 2), sub, jnp.int32(subs), jnp.int32(0)]).astype(I32)

    def swaps(count):
        both = []
        for begin in (0, 1):
            pairs = [(i, i + 1) for i in range(begin, count - 1, 2)]
            both.append(pairs + [(b, a) for a, b in pairs])
        return both

    tile_a, tile_b = swaps(tiles)
    sub_1, sub_2 = swaps(subs)

    def trade(edge_a, edge_b):
        got_b = lax.ppermute(edge_b, "tile", tile_b)
        got_a = lax.ppermute(edge_a, "tile", tile_a)
        return got_a, got_b

    rhs = right_side.reshape(640, 128)
    inverse = fine_inverse.reshape(400, 128)
    coeffs = fine_coeffs.reshape(2000, 128)
    slab, edge, small, cvec = (SLABS * FC, 128), (EDGE, 128), (40, 128), (FC, 128)
    shifts = [(5 * SLABS * FC, 128)]

    (packed,) = call(pack_kernel, [(PACKED, 128)], [meta, rhs, inverse, coeffs, aggregate])
    got_1 = lax.ppermute(packed, "sub", sub_1)
    got_2 = lax.ppermute(packed, "sub", sub_2)
    coeffs_x, inverse_x, rhs_x, index_s, first, edge_a, edge_b = call(
        first_kernel,
        [(SLABS * NIJ, 128), (SLABS * IJ, 128), slab, (8, 128), slab, edge, edge],
        [meta, rhs, inverse, coeffs, got_1, got_2],
    )
    got = trade(edge_a, edge_b)
    smoothed, edge_a, edge_b = call(
        smooth_kernel, [slab, edge, edge], [meta, coeffs_x, inverse_x, rhs_x, first, *got], shifts
    )
    got = trade(edge_a, edge_b)
    residual, scaled, edge_a, edge_b = call(
        residual_kernel, [slab, slab, edge, edge], [meta, coeffs_x, inverse_x, rhs_x, smoothed, *got], shifts
    )
    got = trade(edge_a, edge_b)
    (summed,) = call(
        gather_kernel, [(4, 80, 128)], [meta, coeffs_x, residual, scaled, aggregate, *got], shifts + [(4 * FC, 128)]
    )
    summed = lax.all_to_all(summed, "sub", 0, 0)
    group_rhs, level, coeffs_l, inverse_l, out_a, out_b = call(
        coarse_start_kernel,
        [cvec, cvec, (5, 10, 10, 128), (10, 10, 128), small, small],
        [meta, summed, coarse_coeffs, coarse_inverse, send_rows],
    )
    for _ in range(CSWEEP - 2):
        got = trade(out_a, out_b)
        level, out_a, out_b = call(
            sweep_kernel,
            [cvec, small, small],
            [meta, coeffs_l, inverse_l, coarse_cols, send_rows, group_rhs, level, *got],
        )
    got = trade(out_a, out_b)
    spread, edge_a, edge_b = call(
        last_sweep_kernel,
        [slab, edge, edge],
        [meta, coeffs_l, inverse_l, coarse_cols, group_rhs, level, *got, aggregate, index_s],
    )
    got = trade(edge_a, edge_b)
    applied, scaled, edge_a, edge_b = call(
        correct_kernel, [slab, slab, edge, edge], [meta, coeffs_x, inverse_x, spread, *got], shifts
    )
    got = trade(edge_a, edge_b)
    (out,) = call(
        last_kernel,
        [(640, 128)],
        [meta, coeffs_x, inverse_x, smoothed, residual, spread, applied, scaled, *got],
        shifts,
    )
    return out.reshape(right_side.shape)


def solution(mesh):
    in_specs = (
        P(None, None, "tile", "sub"),
        P(None, None, None, "tile", "sub"),
        P(None, None, "tile", "sub"),
        P("tile", "sub"),
        P(None, None, None, "tile"),
        P(None, None, "tile"),
        P(None, "tile"),
        P(None, "tile"),
    )
    out_specs = P(None, None, "tile", "sub")
    return jax.shard_map(body, mesh=mesh, in_specs=in_specs, out_specs=out_specs, check_vma=False)
```

```python
import jax
import jax.numpy as jnp
from jax import lax
from jax.experimental import pallas as pl
from jax.experimental.pallas import tpu as pltpu
from jax.sharding import PartitionSpec as P

CSWEEP = 4
OMEGA = 0.7
THETA = 0.6
FC = 160
SLABS = 11
STRIP = 10
NIJ = 504
IJ = 104
RAW_J = 3 * FC
RAW_A = RAW_J + 3 * IJ
RAW_G = RAW_A + 2 * NIJ
RAW = RAW_G + 8
F32 = jnp.float32
I32 = jnp.int32
MIB = 1024 * 1024

VM = pl.BlockSpec(memory_space=pltpu.VMEM)
HBM = pl.BlockSpec(memory_space=pltpu.HBM)


def lanes():
    return lax.broadcasted_iota(I32, (8, 128), 1)


def roll(value, shift):
    shift = shift % 128
    return pltpu.roll(value, shift, 1) if shift else value


def pick(value, index):
    return jnp.take_along_axis(value, index, axis=1, mode="promise_in_bounds")


def row(ref, at):
    return jnp.broadcast_to(ref[pl.ds(at, 1), :], (8, 128))


def spread_row(ref, at):
    return jnp.broadcast_to(ref[pl.ds(at, 1), :], (8, 128))


def odd_tile():
    return lax.rem(lax.axis_index("tile"), 2)


def call(kernel, outs, args, scratch=(), specs=None, limit=24):
    def shape(s):
        return s if isinstance(s, jax.ShapeDtypeStruct) else jax.ShapeDtypeStruct(s, F32)

    return pl.pallas_call(
        kernel,
        out_shape=[shape(s) for s in outs],
        in_specs=specs or [VM] * len(args),
        out_specs=[VM] * len(outs),
        scratch_shapes=[pltpu.VMEM(s, F32) if isinstance(s, tuple) else s for s in scratch],
        compiler_params=pltpu.CompilerParams(vmem_limit_bytes=limit * MIB),
    )(*args)


def strip_groups():
    groups = []
    for start in range(0, FC, 8):
        groups.append(("r", start))
    for start in list(range(0, 96, 8)) + [92]:
        groups.append(("j", start))
    for start in list(range(0, 496, 8)) + [492]:
        groups.append(("a", start))
    groups.append(("g", 0))
    return groups


GROUPS = strip_groups()
PACKED = (len(GROUPS) + 3) // 4 * 8


def slot_columns(lane):
    slot = lane & 7
    column = jnp.where(slot <= 2, 2 - slot, jnp.where(slot >= 5, 132 - slot, jnp.where(slot == 3, 127, 0)))
    return column


def raw_message(out, at_row, rhs, inverse, coeffs, aggregate):
    for r in range(3):
        for start in range(0, FC, 8):
            out[pl.ds(r * FC + start, 8), :] = rhs[pl.ds(4 * start + at_row + r, 8, stride=4), :]
        for start in list(range(0, 96, 8)) + [92]:
            out[pl.ds(RAW_J + r * IJ + start, 8), :] = inverse[pl.ds(4 * start + at_row + r, 8, stride=4), :]
    for r in range(2):
        for start in list(range(0, 496, 8)) + [492]:
            out[pl.ds(RAW_A + r * NIJ + start, 8), :] = coeffs[pl.ds(4 * start + 2 * at_row + r, 8, stride=4), :]
    first = jnp.where(at_row == 0, aggregate[pl.ds(0, 1), :], aggregate[pl.ds(2, 1), :])
    second = jnp.where(at_row == 0, aggregate[pl.ds(1, 1), :], aggregate[pl.ds(3, 1), :])
    sublane = lax.broadcasted_iota(I32, (8, 128), 0)
    both = jnp.where(sublane == 0, jnp.broadcast_to(first, (8, 128)), jnp.broadcast_to(second, (8, 128)))
    out[pl.ds(RAW_G, 8), :] = both.astype(F32)


def pack_kernel(rhs_in, inverse_in, coeffs_in, aggregate_in, packed_out, rhs, inverse, coeffs, aggregate, sems):
    copies = []
    for k, (source, target) in enumerate(
        ((coeffs_in, coeffs), (rhs_in, rhs), (inverse_in, inverse), (aggregate_in, aggregate))
    ):
        copies.append(pltpu.make_async_copy(source, target, sems.at[k]))
    for copy in copies:
        copy.start()
    for copy in copies:
        copy.wait()
    lane = lanes()
    index = slot_columns(lane)
    window = lane >> 3
    sources = {"r": rhs, "j": inverse, "a": coeffs}
    for q in range(PACKED // 8):
        packed = jnp.zeros((8, 128), F32)
        for k, (kind, start) in enumerate(GROUPS[4 * q : 4 * q + 4]):
            for x in range(4):
                if kind == "g":
                    block = jnp.broadcast_to(aggregate[pl.ds(x, 1), :].astype(F32), (8, 128))
                else:
                    block = sources[kind][pl.ds(4 * start + x, 8, stride=4), :]
                packed = jnp.where(window == 4 * k + x, pick(block, index), packed)
        packed_out[pl.ds(8 * q, 8), :] = packed


def raw_kernel(packed, rhs, inverse, coeffs, aggregate, raw_b, raw_a):
    odd = odd_tile()
    raw_message(raw_b, odd, rhs, inverse, coeffs, aggregate)
    raw_message(raw_a, 1 - odd, rhs, inverse, coeffs, aggregate)


def merge_kernel(got_1, got_2, mine):
    lane = lanes()
    slot = lane & 7
    odd = lax.rem(lax.axis_index("sub"), 2) == 1
    for q in range(PACKED // 8):
        one, two = got_1[pl.ds(8 * q, 8), :], got_2[pl.ds(8 * q, 8), :]
        left, right = jnp.where(odd, one, two), jnp.where(odd, two, one)
        mine[pl.ds(8 * q, 8), :] = jnp.where(slot <= 2, right, jnp.where(slot >= 5, left, 0.0))


def block_rows(coeff_row, vectors):
    out = []
    for i in range(10):
        pair = None
        for j in range(10):
            m = coeff_row(i, j)
            if pair is None:
                pair = [m * vectors[2 * j], m * vectors[2 * j + 1]]
            else:
                pair = [pair[0] + m * vectors[2 * j], pair[1] + m * vectors[2 * j + 1]]
        out += pair
    return out


def load_slab(ref, base):
    return [ref[pl.ds(base + 8 * b, 8), :] for b in range(20)]


def store_slab(ref, base, values):
    for b in range(20):
        ref[pl.ds(base + 8 * b, 8), :] = values[b]


def at_slab(x):
    return x * FC if isinstance(x, int) else pl.multiple_of(x * FC, 8)


def inverse_at(inverse, x, vectors):
    base = x * IJ if isinstance(x, int) else pl.multiple_of(x * IJ, 8)
    return block_rows(lambda i, j: row(inverse, base + (10 * i + j)), vectors)


def neighbour(source, x, n):
    base = at_slab(x)
    if isinstance(x, int) and x == STRIP:
        shift = (0, 8, -8, -1, 1)[n]
        return [roll(v, shift) for v in load_slab(source, base)]
    if n < 3:
        return load_slab(source, base + (0, -FC, FC)[n])
    lane = lanes()
    out = []
    for b in range(20):
        value = source[pl.ds(base + 8 * b, 8), :]
        strip = source[pl.ds(STRIP * FC + 8 * b, 8), :]
        if n == 3:
            out.append(jnp.where(lane == 0, pltpu.roll(strip, 123 - 8 * x, 1), roll(value, 1)))
        else:
            out.append(jnp.where(lane == 127, pltpu.roll(strip, 125 - 8 * x, 1), roll(value, -1)))
    return out


def stencil_at(coeffs, source, x):
    total = None
    if isinstance(x, int):
        base = 8 * NIJ
    else:
        base = pl.multiple_of((x - 1) * NIJ, 8)
    for n in range(5):
        vectors = neighbour(source, x, n)
        part = block_rows(lambda i, j: row(coeffs, base + (100 * n + 10 * i + j)), vectors)
        total = part if total is None else [a + b for a, b in zip(total, part)]
    return total


def copy_columns(ref, x, values):
    lane = lanes()
    own = (lane == 8 * x + 3) | (lane == 8 * x + 4)
    for b in range(20):
        at = pl.ds(STRIP * FC + 8 * b, 8)
        ref[at, :] = jnp.where(own, pltpu.roll(values[b], 8 * x + 4, 1), ref[at, :])


def over(low, high, step):
    step(STRIP)

    def at(x, carry):
        step(x)
        return carry

    lax.fori_loop(low, high + 1, at, 0)


def down_kernel(
    rhs, inverse, coeffs, aggregate, mine, raw_b, raw_a, strip_a, strip_b,
    coeffs_x, inverse_x, smoothed, residual, index_s, index_t, out,
    rhs_x, first, scaled, filtered,
):
    lane = lanes()
    slot = lane & 7
    odd = odd_tile() == 1
    needed = (lane >= 8) & (lane < 72) & ((slot == 1) | (slot == 2) | (slot == 5) | (slot == 6))
    for q in range(PACKED // 8):
        at = pl.ds(8 * q, 8)
        a, b, own = strip_a[at, :], strip_b[at, :], mine[at, :]
        before, after = jnp.where(odd, a, b), jnp.where(odd, b, a)
        for k, (kind, start) in enumerate(GROUPS[4 * q : 4 * q + 4]):
            placed = jnp.where(
                lane < 24,
                roll(before, -32 * k - 8),
                jnp.where(lane < 56, roll(own, 24 - 32 * k), roll(after, 56 - 32 * k)),
            )
            if kind == "r":
                rhs_x[pl.ds(STRIP * FC + start, 8), :] = jnp.where(lane < 80, placed, 0.0)
            elif kind == "j":
                inverse_x[pl.ds(STRIP * IJ + start, 8), :] = jnp.where(lane < 80, placed, 0.0)
            elif kind == "a":
                coeffs_x[pl.ds(8 * NIJ + start, 8), :] = jnp.where(needed, placed, 0.0)
            else:
                index_s[...] = jnp.where(lane < 80, placed, 0.0)
    for x in range(4):
        for kind, start in GROUPS:
            at = pl.ds(4 * start + x, 8, stride=4)
            if kind == "r":
                rhs_x[pl.ds((x + 3) * FC + start, 8), :] = rhs[at, :]
            elif kind == "j":
                inverse_x[pl.ds((x + 3) * IJ + start, 8), :] = inverse[at, :]
            elif kind == "a":
                coeffs_x[pl.ds((x + 2) * NIJ + start, 8), :] = coeffs[at, :]

    def outer(at_raw, count, ref, at_before, at_after):
        for start in range(0, count, 8):
            a, b = raw_a[pl.ds(at_raw + start, 8), :], raw_b[pl.ds(at_raw + start, 8), :]
            ref[pl.ds(at_before + start, 8), :] = jnp.where(odd, a, b)
            ref[pl.ds(at_after + start, 8), :] = jnp.where(odd, b, a)

    outer(0, 3 * FC, rhs_x, 0, 7 * FC)
    outer(RAW_J, 3 * IJ, inverse_x, 0, 7 * IJ)
    outer(RAW_A, 2 * NIJ, coeffs_x, 0, 6 * NIJ)
    a, b = raw_a[pl.ds(RAW_G, 8), :], raw_b[pl.ds(RAW_G, 8), :]
    sublane = lax.broadcasted_iota(I32, (8, 128), 0)
    after = jnp.where(odd, b, a)
    index_t[...] = jnp.where(sublane < 2, jnp.where(odd, a, b), pltpu.roll(after, 2, 0))

    def start_step(x):
        values = [OMEGA * v for v in inverse_at(inverse_x, x, load_slab(rhs_x, at_slab(x)))]
        store_slab(first, at_slab(x), values)
        if not isinstance(x, int):
            copy_columns(first, x, values)

    over(0, 9, start_step)

    def smooth_step(x):
        base = at_slab(x)
        total = stencil_at(coeffs_x, first, x)
        left = [r - t for r, t in zip(load_slab(rhs_x, base), total)]
        step = inverse_at(inverse_x, x, left)
        values = [v + OMEGA * s for v, s in zip(load_slab(first, base), step)]
        store_slab(smoothed, base, values)
        if not isinstance(x, int):
            copy_columns(smoothed, x, values)

    over(1, 8, smooth_step)

    def residual_step(x):
        base = at_slab(x)
        total = stencil_at(coeffs_x, smoothed, x)
        store_slab(residual, base, [r - t for r, t in zip(load_slab(rhs_x, base), total)])
        store_slab(scaled, base, inverse_at(inverse_x, x, load_slab(residual, base)))

    over(2, 7, residual_step)

    def filter_step(x, carry):
        base = at_slab(x)
        total = stencil_at(coeffs_x, scaled, x)
        store_slab(filtered, at_slab(x - 3), [r - THETA * t for r, t in zip(load_slab(residual, base), total)])
        return carry

    lax.fori_loop(3, 7, filter_step, 0)
    member = lax.broadcasted_iota(I32, (128, 128), 0) & 63
    summed = jnp.zeros((FC, 128), F32)
    for x in range(4):
        owner = jnp.broadcast_to(aggregate[pl.ds(x, 1), :], (128, 128))
        table = (owner == member).astype(F32).astype(jnp.bfloat16)
        rest = filtered[pl.ds(x * FC, FC), :]
        for _ in range(3):
            part = rest.astype(jnp.bfloat16)
            rest = rest - part.astype(F32)
            summed = summed + lax.dot_general(
                part, table, (((1,), (1,)), ((), ())), preferred_element_type=F32
            )
    low = lax.broadcasted_iota(I32, (80, 128), 1) < 64
    packed = jnp.where(low, summed[:80], summed[80:])
    for s in range(4):
        out[s] = packed


def live_lane(index):
    lane = jnp.where(index < 96, index, jnp.where(index < 192, index - 32, index - 80))
    return jnp.where(index >= 256, index - 128, lane)


def live(low, high, lane):
    return jnp.where(lane < 96, low, jnp.where(lane < 112, roll(high, 96), roll(high, 48)))


def send_coarse(index, level, out_a, out_b):
    lane = lanes()
    odd = odd_tile() == 1
    tables = []
    for d in range(2):
        four = jnp.concatenate([index[pl.ds(d, 1), :]] * 4, axis=1)
        tables.append(jnp.broadcast_to(live_lane(four), (8, 128)))
    for out, table in (
        (out_a, jnp.where(odd, tables[0], tables[1])),
        (out_b, jnp.where(odd, tables[1], tables[0])),
    ):
        for g in range(5):
            packed = jnp.zeros((8, 128), F32)
            for k in range(4):
                value = pick(level[pl.ds(8 * (4 * g + k), 8), :], table)
                packed = jnp.where((lane >> 5) == k, value, packed)
            out[pl.ds(8 * g, 8), :] = packed


def coarse_start_kernel(got, coeffs, inverse, send, rhs, level, coeffs_l, inverse_l, out_a, out_b):
    lane = lanes()
    for b in range(20):
        r = 8 * (b % 10)
        up = 64 * (b // 10)
        part = [got[s, pl.ds(r, 8), :] for s in range(4)]
        value = jnp.where(lane < 64, roll(part[0], -up), roll(part[1], 64 - up))
        value = jnp.where(lane < 96, value, jnp.where(lane < 112, roll(part[2], 96 - up), roll(part[3], 112 - up)))
        rhs[pl.ds(8 * b, 8), :] = value
    lane10 = lax.broadcasted_iota(I32, (10, 128), 1)
    for i in range(10):
        inverse_l[i] = live(inverse[i, :, 0:128], inverse[i, :, 128:256], lane10)
    for n in range(5):
        for i in range(10):
            coeffs_l[n, i] = live(coeffs[n, i, :, 0:128], coeffs[n, i, :, 128:256], lane10)
    values = block_rows(lambda i, j: jnp.broadcast_to(inverse_l[i, pl.ds(j, 1), :], (8, 128)), load_slab(rhs, 0))
    store_slab(level, 0, [OMEGA * v for v in values])
    send_coarse(send, level, out_a, out_b)


def sweep(coeffs_l, inverse_l, cols, rhs, level, got_a, got_b):
    lane = lanes()
    odd = odd_tile() == 1
    extra = []
    for g in range(5):
        a, b = got_a[pl.ds(8 * g, 8), :], got_b[pl.ds(8 * g, 8), :]
        before, after = jnp.where(odd, a, b), jnp.where(odd, b, a)
        for k in range(4):
            extra.append(jnp.where(lane < 32, roll(before, -32 * k), roll(after, 32 - 32 * k)))
    total = block_rows(lambda i, j: jnp.broadcast_to(coeffs_l[0, i, pl.ds(j, 1), :], (8, 128)), load_slab(level, 0))
    for n in range(1, 5):
        low, high = cols[pl.ds(n, 1), 0:128], cols[pl.ds(n, 1), 128:256]
        lane1 = lax.broadcasted_iota(I32, (8, 128), 1)
        index = live(jnp.broadcast_to(low, (8, 128)), jnp.broadcast_to(high, (8, 128)), lane1)
        index = live_lane(index)
        near = index & 127
        vectors = []
        for b in range(20):
            own = pick(level[pl.ds(8 * b, 8), :], near)
            vectors.append(jnp.where(index < 128, own, pick(extra[b], near)))
        part = block_rows(lambda i, j: jnp.broadcast_to(coeffs_l[n, i, pl.ds(j, 1), :], (8, 128)), vectors)
        total = [a + b for a, b in zip(total, part)]
    left = [r - t for r, t in zip(load_slab(rhs, 0), total)]
    step = block_rows(lambda i, j: jnp.broadcast_to(inverse_l[i, pl.ds(j, 1), :], (8, 128)), left)
    return [v + OMEGA * s for v, s in zip(load_slab(level, 0), step)]


def sweep_kernel(coeffs_l, inverse_l, cols, send, rhs, level, got_b, got_a, out, out_b, out_a):
    store_slab(out, 0, sweep(coeffs_l, inverse_l, cols, rhs, level, got_a, got_b))
    send_coarse(send, out, out_a, out_b)


def last_sweep_kernel(coeffs_l, inverse_l, cols, rhs, level, got_b, got_a, out):
    store_slab(out, 0, sweep(coeffs_l, inverse_l, cols, rhs, level, got_a, got_b))


def up_kernel(
    coeffs_x, inverse_x, smoothed, residual, aggregate, index_s, index_t, level, got_a, got_b,
    out, spread, applied, scaled,
):
    lane = lanes()
    slot = lane & 7
    odd = odd_tile() == 1
    sub, subs = lax.axis_index("sub"), lax.axis_size("sub")

    def offset(s):
        return jnp.where(s <= 0, 0, jnp.where(s == 1, 64, jnp.where(s == 2, 96, 112)))

    own_at = offset(sub)
    mains = [jnp.minimum(jnp.broadcast_to(aggregate[pl.ds(x, 1), :], (8, 128)) + own_at, 127) for x in range(4)]
    outers = [jnp.minimum(spread_row(index_t, r).astype(I32) + own_at, 127) for r in range(4)]
    side = jnp.where(slot <= 2, offset(sub + 1), offset(sub - 1))
    beside = jnp.minimum(index_s[...].astype(I32) + side, 127)
    there = ((slot <= 2) & (sub < subs - 1)) | ((slot >= 5) & (sub > 0))
    for b in range(20):
        at = pl.ds(8 * b, 8)
        own, va, vb = level[at, :], got_a[at, :], got_b[at, :]
        before, after = jnp.where(odd, va, vb), jnp.where(odd, vb, va)
        strip = jnp.where(
            lane < 24, pick(before, beside), jnp.where(lane < 56, pick(own, beside), pick(after, beside))
        )
        strip = jnp.where(there & (lane < 80), strip, 0.0)
        for x in range(1, 9):
            if x < 3:
                value = pick(before, outers[x - 1])
            elif x < 7:
                value = pick(own, mains[x - 3])
            else:
                value = pick(after, outers[x - 5])
            spread[pl.ds(x * FC + 8 * b, 8), :] = value
            strip = jnp.where((lane == 8 * x + 3) | (lane == 8 * x + 4), roll(value, 8 * x + 4), strip)
        spread[pl.ds(STRIP * FC + 8 * b, 8), :] = strip

    def spread_step(x):
        base = at_slab(x)
        store_slab(applied, base, stencil_at(coeffs_x, spread, x))
        store_slab(scaled, base, inverse_at(inverse_x, x, load_slab(applied, base)))

    over(2, 7, spread_step)

    def last_step(x, carry):
        base = at_slab(x)
        total = stencil_at(coeffs_x, scaled, x)
        left = [
            r - a + THETA * t
            for r, a, t in zip(load_slab(residual, base), load_slab(applied, base), total)
        ]
        step = inverse_at(inverse_x, x, left)
        for b in range(20):
            at = pl.ds(base + 8 * b, 8)
            value = smoothed[at, :] + spread[at, :] - THETA * scaled[at, :] + OMEGA * step[b]
            out[pl.ds(32 * b + x - 3, 8, stride=4), :] = value
        return carry

    lax.fori_loop(3, 7, last_step, 0)


def body(right_side, fine_coeffs, fine_inverse, aggregate, coarse_coeffs, coarse_inverse, coarse_cols, send_rows):
    tiles, subs = lax.axis_size("tile"), lax.axis_size("sub")

    def swaps(count):
        both = []
        for begin in (0, 1):
            pairs = [(i, i + 1) for i in range(begin, count - 1, 2)]
            both.append(pairs + [(b, a) for a, b in pairs])
        return both

    tile_a, tile_b = swaps(tiles)
    sub_1, sub_2 = swaps(subs)

    def trade(to_b, to_a):
        return lax.ppermute(to_b, "tile", tile_b), lax.ppermute(to_a, "tile", tile_a)

    rhs = right_side.reshape(640, 128)
    inverse = fine_inverse.reshape(400, 128)
    coeffs = fine_coeffs.reshape(2000, 128)
    slabs, small, cvec = (SLABS * FC, 128), (40, 128), (FC, 128)
    copy = jax.ShapeDtypeStruct

    packed, rhs, inverse, coeffs, aggregate = call(
        pack_kernel,
        [(PACKED, 128), (640, 128), (400, 128), (2000, 128), copy((4, 128), I32)],
        [rhs, inverse, coeffs, aggregate],
        [pltpu.SemaphoreType.DMA((4,))],
        [HBM] * 4,
        48,
    )
    got_1 = lax.ppermute(packed, "sub", sub_1)
    got_2 = lax.ppermute(packed, "sub", sub_2)
    raw_b, raw_a = call(raw_kernel, [(RAW, 128), (RAW, 128)], [packed, rhs, inverse, coeffs, aggregate])
    raw = trade(raw_b, raw_a)
    (mine,) = call(merge_kernel, [(PACKED, 128)], [got_1, got_2])
    strips = trade(mine, mine)[::-1]
    coeffs_x, inverse_x, smoothed, residual, index_s, index_t, summed = call(
        down_kernel,
        [(9 * NIJ, 128), (SLABS * IJ, 128), slabs, slabs, (8, 128), (8, 128), (4, 80, 128)],
        [rhs, inverse, coeffs, aggregate, mine, *raw, *strips],
        [slabs, slabs, slabs, (4 * FC, 128)],
    )
    summed = lax.all_to_all(summed, "sub", 0, 0)
    group_rhs, level, coeffs_l, inverse_l, out_a, out_b = call(
        coarse_start_kernel,
        [cvec, cvec, (5, 10, 10, 128), (10, 10, 128), small, small],
        [summed, coarse_coeffs, coarse_inverse, send_rows],
    )
    for _ in range(CSWEEP - 2):
        level, out_b, out_a = call(
            sweep_kernel,
            [cvec, small, small],
            [coeffs_l, inverse_l, coarse_cols, send_rows, group_rhs, level, *trade(out_b, out_a)],
        )
    (level,) = call(
        last_sweep_kernel,
        [cvec],
        [coeffs_l, inverse_l, coarse_cols, group_rhs, level, *trade(out_b, out_a)],
    )
    (out,) = call(
        up_kernel,
        [(640, 128)],
        [coeffs_x, inverse_x, smoothed, residual, aggregate, index_s, index_t, level, *trade(level, level)[::-1]],
        [slabs, slabs, slabs],
    )
    return out.reshape(right_side.shape)


def solution(mesh):
    in_specs = (
        P(None, None, "tile", "sub"),
        P(None, None, None, "tile", "sub"),
        P(None, None, "tile", "sub"),
        P("tile", "sub"),
        P(None, None, None, "tile"),
        P(None, None, "tile"),
        P(None, "tile"),
        P(None, "tile"),
    )
    out_specs = P(None, None, "tile", "sub")
    return jax.shard_map(body, mesh=mesh, in_specs=in_specs, out_specs=out_specs, check_vma=False)
```

```python
import jax
import jax.numpy as jnp
from jax import lax
from jax.experimental import pallas as pl
from jax.experimental.pallas import tpu as pltpu
from jax.sharding import PartitionSpec as P

CSWEEP = 4
OMEGA = 0.7
THETA = 0.6
FC = 160
SLABS = 11
STRIP = 10
NIJ = 504
IJ = 104
RAW_J = 3 * FC
RAW_A = RAW_J + 3 * IJ
RAW_G = RAW_A + 2 * NIJ
RAW = RAW_G + 8
F32 = jnp.float32
I32 = jnp.int32
MIB = 1024 * 1024

VM = pl.BlockSpec(memory_space=pltpu.VMEM)
HBM = pl.BlockSpec(memory_space=pltpu.HBM)


def lanes():
    return lax.broadcasted_iota(I32, (8, 128), 1)


def roll(value, shift):
    shift = shift % 128
    return pltpu.roll(value, shift, 1) if shift else value


def pick(value, index):
    return jnp.take_along_axis(value, index, axis=1, mode="promise_in_bounds")


def row(ref, at):
    return jnp.broadcast_to(ref[pl.ds(at, 1), :], (8, 128))


def spread_row(ref, at):
    return jnp.broadcast_to(ref[pl.ds(at, 1), :], (8, 128))


def odd_tile():
    return lax.rem(lax.axis_index("tile"), 2)


def call(kernel, outs, args, scratch=(), specs=None, limit=24):
    def shape(s):
        return s if isinstance(s, jax.ShapeDtypeStruct) else jax.ShapeDtypeStruct(s, F32)

    return pl.pallas_call(
        kernel,
        out_shape=[shape(s) for s in outs],
        in_specs=specs or [VM] * len(args),
        out_specs=[VM] * len(outs),
        scratch_shapes=[pltpu.VMEM(s, F32) if isinstance(s, tuple) else s for s in scratch],
        compiler_params=pltpu.CompilerParams(vmem_limit_bytes=limit * MIB),
    )(*args)


def strip_groups():
    groups = []
    for start in range(0, FC, 8):
        groups.append(("r", start))
    for start in list(range(0, 96, 8)) + [92]:
        groups.append(("j", start))
    for start in list(range(0, 496, 8)) + [492]:
        groups.append(("a", start))
    groups.append(("g", 0))
    return groups


GROUPS = strip_groups()
PACKED = (len(GROUPS) + 3) // 4 * 8


def slot_columns(lane):
    slot = lane & 7
    column = jnp.where(slot <= 2, 2 - slot, jnp.where(slot >= 5, 132 - slot, jnp.where(slot == 3, 127, 0)))
    return column


def raw_message(out, at_row, rhs, inverse, coeffs, aggregate):
    for r in range(3):
        for start in range(0, FC, 8):
            out[pl.ds(r * FC + start, 8), :] = rhs[pl.ds(4 * start + at_row + r, 8, stride=4), :]
        for start in list(range(0, 96, 8)) + [92]:
            out[pl.ds(RAW_J + r * IJ + start, 8), :] = inverse[pl.ds(4 * start + at_row + r, 8, stride=4), :]
    for r in range(2):
        for start in list(range(0, 496, 8)) + [492]:
            out[pl.ds(RAW_A + r * NIJ + start, 8), :] = coeffs[pl.ds(4 * start + 2 * at_row + r, 8, stride=4), :]
    first = jnp.where(at_row == 0, aggregate[pl.ds(0, 1), :], aggregate[pl.ds(2, 1), :])
    second = jnp.where(at_row == 0, aggregate[pl.ds(1, 1), :], aggregate[pl.ds(3, 1), :])
    sublane = lax.broadcasted_iota(I32, (8, 128), 0)
    both = jnp.where(sublane == 0, jnp.broadcast_to(first, (8, 128)), jnp.broadcast_to(second, (8, 128)))
    out[pl.ds(RAW_G, 8), :] = both


class Rows:
    def __init__(self, ref, first):
        self.ref, self.first = ref, first

    def __getitem__(self, index):
        rows, columns = index
        return self.ref[pl.ds(rows.start + self.first, rows.size, stride=rows.stride), columns]


def parts(whole):
    return [Rows(whole, first) for first in (0, 640, 1040, 3040)]


def pack_kernel(whole, packed_out):
    rhs, inverse, coeffs, aggregate = parts(whole)
    lane = lanes()
    index = slot_columns(lane)
    window = lane >> 3
    sources = {"r": rhs, "j": inverse, "a": coeffs}
    for q in range(PACKED // 8):
        packed = jnp.zeros((8, 128), F32)
        for k, (kind, start) in enumerate(GROUPS[4 * q : 4 * q + 4]):
            for x in range(4):
                if kind == "g":
                    block = jnp.broadcast_to(aggregate[pl.ds(x, 1), :], (8, 128))
                else:
                    block = sources[kind][pl.ds(4 * start + x, 8, stride=4), :]
                packed = jnp.where(window == 4 * k + x, pick(block, index), packed)
        packed_out[pl.ds(8 * q, 8), :] = packed


def raw_kernel(packed, whole, raw_b, raw_a):
    rhs, inverse, coeffs, aggregate = parts(whole)
    odd = odd_tile()
    raw_message(raw_b, odd, rhs, inverse, coeffs, aggregate)
    raw_message(raw_a, 1 - odd, rhs, inverse, coeffs, aggregate)


def merge_kernel(got_1, got_2, mine):
    lane = lanes()
    slot = lane & 7
    odd = lax.rem(lax.axis_index("sub"), 2) == 1
    for q in range(PACKED // 8):
        one, two = got_1[pl.ds(8 * q, 8), :], got_2[pl.ds(8 * q, 8), :]
        left, right = jnp.where(odd, one, two), jnp.where(odd, two, one)
        mine[pl.ds(8 * q, 8), :] = jnp.where(slot <= 2, right, jnp.where(slot >= 5, left, 0.0))


def block_rows(coeff_row, vectors):
    out = []
    for i in range(10):
        pair = None
        for j in range(10):
            m = coeff_row(i, j)
            if pair is None:
                pair = [m * vectors[2 * j], m * vectors[2 * j + 1]]
            else:
                pair = [pair[0] + m * vectors[2 * j], pair[1] + m * vectors[2 * j + 1]]
        out += pair
    return out


def load_slab(ref, base):
    return [ref[pl.ds(base + 8 * b, 8), :] for b in range(20)]


def store_slab(ref, base, values):
    for b in range(20):
        ref[pl.ds(base + 8 * b, 8), :] = values[b]


def at_slab(x):
    return x * FC if isinstance(x, int) else pl.multiple_of(x * FC, 8)


def inverse_at(inverse, x, vectors):
    base = x * IJ if isinstance(x, int) else pl.multiple_of(x * IJ, 8)
    return block_rows(lambda i, j: row(inverse, base + (10 * i + j)), vectors)


def neighbour(source, x, n):
    base = at_slab(x)
    if isinstance(x, int) and x == STRIP:
        shift = (0, 8, -8, -1, 1)[n]
        return [roll(v, shift) for v in load_slab(source, base)]
    if n < 3:
        return load_slab(source, base + (0, -FC, FC)[n])
    lane = lanes()
    out = []
    for b in range(20):
        value = source[pl.ds(base + 8 * b, 8), :]
        strip = source[pl.ds(STRIP * FC + 8 * b, 8), :]
        if n == 3:
            out.append(jnp.where(lane == 0, pltpu.roll(strip, 123 - 8 * x, 1), roll(value, 1)))
        else:
            out.append(jnp.where(lane == 127, pltpu.roll(strip, 125 - 8 * x, 1), roll(value, -1)))
    return out


def stencil_at(coeffs, source, x, moved):
    total = None
    if isinstance(x, int):
        base = 8 * NIJ
    else:
        base = pl.multiple_of((x - 1) * NIJ, 8)
    through = range(1, 5) if isinstance(x, int) else range(3, 5)
    for n in through:
        store_slab(moved, (n - 1) * FC, neighbour(source, x, n))
    for n in range(5):
        vectors = load_slab(moved, (n - 1) * FC) if n in through else neighbour(source, x, n)
        part = block_rows(lambda i, j: row(coeffs, base + (100 * n + 10 * i + j)), vectors)
        total = part if total is None else [a + b for a, b in zip(total, part)]
    return total


def copy_columns(ref, x, values):
    lane = lanes()
    own = (lane == 8 * x + 3) | (lane == 8 * x + 4)
    for b in range(20):
        at = pl.ds(STRIP * FC + 8 * b, 8)
        ref[at, :] = jnp.where(own, pltpu.roll(values[b], 8 * x + 4, 1), ref[at, :])


def over(low, high, step):
    step(STRIP)

    def at(x, carry):
        step(x)
        return carry

    lax.fori_loop(low, high + 1, at, 0)


def down_kernel(
    whole, mine, raw_b, raw_a, strip_a, strip_b,
    coeffs_x, inverse_x, smoothed, residual, index_s, index_t, out,
    rhs_x, first, scaled, filtered, moved,
):
    lane = lanes()
    slot = lane & 7
    rhs, inverse, coeffs, aggregate = parts(whole)
    odd = odd_tile() == 1
    needed = (lane >= 8) & (lane < 72) & ((slot == 1) | (slot == 2) | (slot == 5) | (slot == 6))
    for q in range(PACKED // 8):
        at = pl.ds(8 * q, 8)
        a, b, own = strip_a[at, :], strip_b[at, :], mine[at, :]
        before, after = jnp.where(odd, a, b), jnp.where(odd, b, a)
        for k, (kind, start) in enumerate(GROUPS[4 * q : 4 * q + 4]):
            placed = jnp.where(
                lane < 24,
                roll(before, -32 * k - 8),
                jnp.where(lane < 56, roll(own, 24 - 32 * k), roll(after, 56 - 32 * k)),
            )
            if kind == "r":
                rhs_x[pl.ds(STRIP * FC + start, 8), :] = jnp.where(lane < 80, placed, 0.0)
            elif kind == "j":
                inverse_x[pl.ds(STRIP * IJ + start, 8), :] = jnp.where(lane < 80, placed, 0.0)
            elif kind == "a":
                coeffs_x[pl.ds(8 * NIJ + start, 8), :] = jnp.where(needed, placed, 0.0)
            else:
                index_s[...] = jnp.where(lane < 80, placed, 0.0)
    for x in range(4):
        for kind, start in GROUPS:
            at = pl.ds(4 * start + x, 8, stride=4)
            if kind == "r":
                rhs_x[pl.ds((x + 3) * FC + start, 8), :] = rhs[at, :]
            elif kind == "j":
                inverse_x[pl.ds((x + 3) * IJ + start, 8), :] = inverse[at, :]
            elif kind == "a":
                coeffs_x[pl.ds((x + 2) * NIJ + start, 8), :] = coeffs[at, :]

    def outer(at_raw, count, ref, at_before, at_after):
        for start in range(0, count, 8):
            a, b = raw_a[pl.ds(at_raw + start, 8), :], raw_b[pl.ds(at_raw + start, 8), :]
            ref[pl.ds(at_before + start, 8), :] = jnp.where(odd, a, b)
            ref[pl.ds(at_after + start, 8), :] = jnp.where(odd, b, a)

    outer(0, 3 * FC, rhs_x, 0, 7 * FC)
    outer(RAW_J, 3 * IJ, inverse_x, 0, 7 * IJ)
    outer(RAW_A, 2 * NIJ, coeffs_x, 0, 6 * NIJ)
    a, b = raw_a[pl.ds(RAW_G, 8), :], raw_b[pl.ds(RAW_G, 8), :]
    sublane = lax.broadcasted_iota(I32, (8, 128), 0)
    after = jnp.where(odd, b, a)
    index_t[...] = jnp.where(sublane < 2, jnp.where(odd, a, b), pltpu.roll(after, 2, 0))

    def start_step(x):
        values = [OMEGA * v for v in inverse_at(inverse_x, x, load_slab(rhs_x, at_slab(x)))]
        if not isinstance(x, int):
            copy_columns(first, x, values)
        store_slab(first, at_slab(x), values)

    over(0, 9, start_step)

    def smooth_step(x):
        base = at_slab(x)
        total = stencil_at(coeffs_x, first, x, moved)
        left = [r - t for r, t in zip(load_slab(rhs_x, base), total)]
        step = inverse_at(inverse_x, x, left)
        values = [v + OMEGA * s for v, s in zip(load_slab(first, base), step)]
        if not isinstance(x, int):
            copy_columns(smoothed, x, values)
        store_slab(smoothed, base, values)

    over(1, 8, smooth_step)

    def residual_step(x):
        base = at_slab(x)
        total = stencil_at(coeffs_x, smoothed, x, moved)
        store_slab(residual, base, [r - t for r, t in zip(load_slab(rhs_x, base), total)])
        store_slab(scaled, base, inverse_at(inverse_x, x, load_slab(residual, base)))

    over(2, 7, residual_step)

    def filter_step(x, carry):
        base = at_slab(x)
        total = stencil_at(coeffs_x, scaled, x, moved)
        store_slab(filtered, at_slab(x - 3), [r - THETA * t for r, t in zip(load_slab(residual, base), total)])
        return carry

    lax.fori_loop(3, 7, filter_step, 0)
    member = lax.broadcasted_iota(I32, (128, 128), 0) & 63
    summed = jnp.zeros((FC, 128), F32)
    for x in range(4):
        owner = jnp.broadcast_to(aggregate[pl.ds(x, 1), :].astype(I32), (128, 128))
        table = (owner == member).astype(F32).astype(jnp.bfloat16)
        rest = filtered[pl.ds(x * FC, FC), :]
        for _ in range(3):
            part = rest.astype(jnp.bfloat16)
            rest = rest - part.astype(F32)
            summed = summed + lax.dot_general(
                part, table, (((1,), (1,)), ((), ())), preferred_element_type=F32
            )
    low = lax.broadcasted_iota(I32, (80, 128), 1) < 64
    packed = jnp.where(low, summed[:80], summed[80:])
    for s in range(4):
        out[s] = packed


def live_lane(index):
    lane = jnp.where(index < 96, index, jnp.where(index < 192, index - 32, index - 80))
    return jnp.where(index >= 256, index - 128, lane)


def live(low, high, lane):
    return jnp.where(lane < 96, low, jnp.where(lane < 112, roll(high, 96), roll(high, 48)))


def send_coarse(index, level, out_a, out_b):
    lane = lanes()
    odd = odd_tile() == 1
    tables = []
    for d in range(2):
        four = jnp.concatenate([index[pl.ds(d, 1), :]] * 4, axis=1)
        tables.append(jnp.broadcast_to(live_lane(four), (8, 128)))
    for out, table in (
        (out_a, jnp.where(odd, tables[0], tables[1])),
        (out_b, jnp.where(odd, tables[1], tables[0])),
    ):
        for g in range(5):
            packed = jnp.zeros((8, 128), F32)
            for k in range(4):
                value = pick(level[pl.ds(8 * (4 * g + k), 8), :], table)
                packed = jnp.where((lane >> 5) == k, value, packed)
            out[pl.ds(8 * g, 8), :] = packed


def coarse_start_kernel(got, coeffs, inverse, send, rhs, level, coeffs_l, inverse_l, out_a, out_b):
    lane = lanes()
    for b in range(20):
        r = 8 * (b % 10)
        up = 64 * (b // 10)
        part = [got[s, pl.ds(r, 8), :] for s in range(4)]
        value = jnp.where(lane < 64, roll(part[0], -up), roll(part[1], 64 - up))
        value = jnp.where(lane < 96, value, jnp.where(lane < 112, roll(part[2], 96 - up), roll(part[3], 112 - up)))
        rhs[pl.ds(8 * b, 8), :] = value
    lane10 = lax.broadcasted_iota(I32, (10, 128), 1)
    for i in range(10):
        inverse_l[i] = live(inverse[i, :, 0:128], inverse[i, :, 128:256], lane10)
    for n in range(5):
        for i in range(10):
            coeffs_l[n, i] = live(coeffs[n, i, :, 0:128], coeffs[n, i, :, 128:256], lane10)
    values = block_rows(lambda i, j: jnp.broadcast_to(inverse_l[i, pl.ds(j, 1), :], (8, 128)), load_slab(rhs, 0))
    store_slab(level, 0, [OMEGA * v for v in values])
    send_coarse(send, level, out_a, out_b)


def sweep(coeffs_l, inverse_l, cols, rhs, level, got_a, got_b):
    lane = lanes()
    odd = odd_tile() == 1
    extra = []
    for g in range(5):
        a, b = got_a[pl.ds(8 * g, 8), :], got_b[pl.ds(8 * g, 8), :]
        before, after = jnp.where(odd, a, b), jnp.where(odd, b, a)
        for k in range(4):
            extra.append(jnp.where(lane < 32, roll(before, -32 * k), roll(after, 32 - 32 * k)))
    total = block_rows(lambda i, j: jnp.broadcast_to(coeffs_l[0, i, pl.ds(j, 1), :], (8, 128)), load_slab(level, 0))
    for n in range(1, 5):
        low, high = cols[pl.ds(n, 1), 0:128], cols[pl.ds(n, 1), 128:256]
        lane1 = lax.broadcasted_iota(I32, (8, 128), 1)
        index = live(jnp.broadcast_to(low, (8, 128)), jnp.broadcast_to(high, (8, 128)), lane1)
        index = live_lane(index)
        near = index & 127
        vectors = []
        for b in range(20):
            own = pick(level[pl.ds(8 * b, 8), :], near)
            vectors.append(jnp.where(index < 128, own, pick(extra[b], near)))
        part = block_rows(lambda i, j: jnp.broadcast_to(coeffs_l[n, i, pl.ds(j, 1), :], (8, 128)), vectors)
        total = [a + b for a, b in zip(total, part)]
    left = [r - t for r, t in zip(load_slab(rhs, 0), total)]
    step = block_rows(lambda i, j: jnp.broadcast_to(inverse_l[i, pl.ds(j, 1), :], (8, 128)), left)
    return [v + OMEGA * s for v, s in zip(load_slab(level, 0), step)]


def sweep_kernel(coeffs_l, inverse_l, cols, send, rhs, level, got_b, got_a, out, out_b, out_a):
    store_slab(out, 0, sweep(coeffs_l, inverse_l, cols, rhs, level, got_a, got_b))
    send_coarse(send, out, out_a, out_b)


def last_sweep_kernel(coeffs_l, inverse_l, cols, rhs, level, got_b, got_a, out):
    store_slab(out, 0, sweep(coeffs_l, inverse_l, cols, rhs, level, got_a, got_b))


def up_kernel(
    coeffs_x, inverse_x, smoothed, residual, whole, index_s, index_t, level, got_a, got_b,
    out, spread, applied, scaled, moved,
):
    lane = lanes()
    slot = lane & 7
    odd = odd_tile() == 1
    sub, subs = lax.axis_index("sub"), lax.axis_size("sub")

    def offset(s):
        return jnp.where(s <= 0, 0, jnp.where(s == 1, 64, jnp.where(s == 2, 96, 112)))

    own_at = offset(sub)
    aggregate = parts(whole)[3]
    mains = [jnp.minimum(row(aggregate, x).astype(I32) + own_at, 127) for x in range(4)]
    outers = [jnp.minimum(spread_row(index_t, r).astype(I32) + own_at, 127) for r in range(4)]
    side = jnp.where(slot <= 2, offset(sub + 1), offset(sub - 1))
    beside = jnp.minimum(index_s[...].astype(I32) + side, 127)
    there = ((slot <= 2) & (sub < subs - 1)) | ((slot >= 5) & (sub > 0))
    for b in range(20):
        at = pl.ds(8 * b, 8)
        own, va, vb = level[at, :], got_a[at, :], got_b[at, :]
        before, after = jnp.where(odd, va, vb), jnp.where(odd, vb, va)
        strip = jnp.where(
            lane < 24, pick(before, beside), jnp.where(lane < 56, pick(own, beside), pick(after, beside))
        )
        strip = jnp.where(there & (lane < 80), strip, 0.0)
        for x in range(1, 9):
            if x < 3:
                value = pick(before, outers[x - 1])
            elif x < 7:
                value = pick(own, mains[x - 3])
            else:
                value = pick(after, outers[x - 5])
            spread[pl.ds(x * FC + 8 * b, 8), :] = value
            strip = jnp.where((lane == 8 * x + 3) | (lane == 8 * x + 4), roll(value, 8 * x + 4), strip)
        spread[pl.ds(STRIP * FC + 8 * b, 8), :] = strip

    def spread_step(x):
        base = at_slab(x)
        store_slab(applied, base, stencil_at(coeffs_x, spread, x, moved))
        store_slab(scaled, base, inverse_at(inverse_x, x, load_slab(applied, base)))

    over(2, 7, spread_step)

    def last_step(x, carry):
        base = at_slab(x)
        total = stencil_at(coeffs_x, scaled, x, moved)
        left = [
            r - a + THETA * t
            for r, a, t in zip(load_slab(residual, base), load_slab(applied, base), total)
        ]
        step = inverse_at(inverse_x, x, left)
        for b in range(20):
            at = pl.ds(base + 8 * b, 8)
            value = smoothed[at, :] + spread[at, :] - THETA * scaled[at, :] + OMEGA * step[b]
            out[pl.ds(32 * b + x - 3, 8, stride=4), :] = value
        return carry

    lax.fori_loop(3, 7, last_step, 0)


def body(right_side, fine_coeffs, fine_inverse, aggregate, coarse_coeffs, coarse_inverse, coarse_cols, send_rows):
    tiles, subs = lax.axis_size("tile"), lax.axis_size("sub")

    def swaps(count):
        both = []
        for begin in (0, 1):
            pairs = [(i, i + 1) for i in range(begin, count - 1, 2)]
            both.append(pairs + [(b, a) for a, b in pairs])
        return both

    tile_a, tile_b = swaps(tiles)
    sub_1, sub_2 = swaps(subs)

    def trade(to_b, to_a):
        return lax.ppermute(to_b, "tile", tile_b), lax.ppermute(to_a, "tile", tile_a)

    rhs = right_side.reshape(640, 128)
    inverse = fine_inverse.reshape(400, 128)
    coeffs = fine_coeffs.reshape(2000, 128)
    slabs, small, cvec = (SLABS * FC, 128), (40, 128), (FC, 128)

    whole = jnp.concatenate([rhs, inverse, coeffs, aggregate.astype(F32)], axis=0)
    (packed,) = call(pack_kernel, [(PACKED, 128)], [whole])
    got_1 = lax.ppermute(packed, "sub", sub_1)
    got_2 = lax.ppermute(packed, "sub", sub_2)
    raw_b, raw_a = call(raw_kernel, [(RAW, 128), (RAW, 128)], [packed, whole])
    raw = trade(raw_b, raw_a)
    (mine,) = call(merge_kernel, [(PACKED, 128)], [got_1, got_2])
    strips = trade(mine, mine)[::-1]
    coeffs_x, inverse_x, smoothed, residual, index_s, index_t, summed = call(
        down_kernel,
        [(9 * NIJ, 128), (SLABS * IJ, 128), slabs, slabs, (8, 128), (8, 128), (4, 80, 128)],
        [whole, mine, *raw, *strips],
        [slabs, slabs, slabs, (4 * FC, 128), (4 * FC, 128)],
    )
    summed = lax.all_to_all(summed, "sub", 0, 0)
    group_rhs, level, coeffs_l, inverse_l, out_a, out_b = call(
        coarse_start_kernel,
        [cvec, cvec, (5, 10, 10, 128), (10, 10, 128), small, small],
        [summed, coarse_coeffs, coarse_inverse, send_rows],
    )
    for _ in range(CSWEEP - 2):
        level, out_b, out_a = call(
            sweep_kernel,
            [cvec, small, small],
            [coeffs_l, inverse_l, coarse_cols, send_rows, group_rhs, level, *trade(out_b, out_a)],
        )
    (level,) = call(
        last_sweep_kernel,
        [cvec],
        [coeffs_l, inverse_l, coarse_cols, group_rhs, level, *trade(out_b, out_a)],
    )
    (out,) = call(
        up_kernel,
        [(640, 128)],
        [coeffs_x, inverse_x, smoothed, residual, whole, index_s, index_t, level, *trade(level, level)[::-1]],
        [slabs, slabs, slabs, (4 * FC, 128)],
    )
    return out.reshape(right_side.shape)


def solution(mesh):
    in_specs = (
        P(None, None, "tile", "sub"),
        P(None, None, None, "tile", "sub"),
        P(None, None, "tile", "sub"),
        P("tile", "sub"),
        P(None, None, None, "tile"),
        P(None, None, "tile"),
        P(None, "tile"),
        P(None, "tile"),
    )
    out_specs = P(None, None, "tile", "sub")
    return jax.shard_map(body, mesh=mesh, in_specs=in_specs, out_specs=out_specs, check_vma=False)
```

```python
import jax
import jax.numpy as jnp
from jax import lax
from jax.experimental import pallas as pl
from jax.experimental.pallas import tpu as pltpu
from jax.sharding import PartitionSpec as P

CSWEEP = 4
OMEGA = 0.7
THETA = 0.6
FC = 160
SLABS = 11
STRIP = 10
NIJ = 504
IJ = 104
RAW_J = 3 * FC
RAW_A = RAW_J + 3 * IJ
RAW_G = RAW_A + 2 * NIJ
RAW = RAW_G + 8
F32 = jnp.float32
I32 = jnp.int32
MIB = 1024 * 1024

VM = pl.BlockSpec(memory_space=pltpu.VMEM)
HBM = pl.BlockSpec(memory_space=pltpu.HBM)


def lanes():
    return lax.broadcasted_iota(I32, (8, 128), 1)


def roll(value, shift):
    shift = shift % 128
    return pltpu.roll(value, shift, 1) if shift else value


def pick(value, index):
    return jnp.take_along_axis(value, index, axis=1, mode="promise_in_bounds")


def row(ref, at):
    return jnp.broadcast_to(ref[pl.ds(at, 1), :], (8, 128))


def spread_row(ref, at):
    return jnp.broadcast_to(ref[pl.ds(at, 1), :], (8, 128))


def odd_tile():
    return lax.rem(lax.axis_index("tile"), 2)


def call(kernel, outs, args, scratch=(), specs=None, limit=24):
    def shape(s):
        return s if isinstance(s, jax.ShapeDtypeStruct) else jax.ShapeDtypeStruct(s, F32)

    return pl.pallas_call(
        kernel,
        out_shape=[shape(s) for s in outs],
        in_specs=specs or [VM] * len(args),
        out_specs=[VM] * len(outs),
        scratch_shapes=[pltpu.VMEM(s, F32) if isinstance(s, tuple) else s for s in scratch],
        compiler_params=pltpu.CompilerParams(vmem_limit_bytes=limit * MIB),
    )(*args)


def strip_groups():
    groups = []
    for start in range(0, FC, 8):
        groups.append(("r", start))
    for start in list(range(0, 96, 8)) + [92]:
        groups.append(("j", start))
    for start in list(range(0, 496, 8)) + [492]:
        groups.append(("a", start))
    groups.append(("g", 0))
    return groups


GROUPS = strip_groups()
PACKED = (len(GROUPS) + 3) // 4 * 8


def slot_columns(lane):
    slot = lane & 7
    column = jnp.where(slot <= 2, 2 - slot, jnp.where(slot >= 5, 132 - slot, jnp.where(slot == 3, 127, 0)))
    return column


def raw_message(out, at_row, rhs, inverse, coeffs, aggregate):
    for r in range(3):
        for start in range(0, FC, 8):
            out[pl.ds(r * FC + start, 8), :] = rhs[pl.ds(4 * start + at_row + r, 8, stride=4), :]
        for start in list(range(0, 96, 8)) + [92]:
            out[pl.ds(RAW_J + r * IJ + start, 8), :] = inverse[pl.ds(4 * start + at_row + r, 8, stride=4), :]
    for r in range(2):
        for start in list(range(0, 496, 8)) + [492]:
            out[pl.ds(RAW_A + r * NIJ + start, 8), :] = coeffs[pl.ds(4 * start + 2 * at_row + r, 8, stride=4), :]
    first = jnp.where(at_row == 0, aggregate[pl.ds(0, 1), :], aggregate[pl.ds(2, 1), :])
    second = jnp.where(at_row == 0, aggregate[pl.ds(1, 1), :], aggregate[pl.ds(3, 1), :])
    sublane = lax.broadcasted_iota(I32, (8, 128), 0)
    both = jnp.where(sublane == 0, jnp.broadcast_to(first, (8, 128)), jnp.broadcast_to(second, (8, 128)))
    out[pl.ds(RAW_G, 8), :] = both.astype(F32)


class Rows:
    def __init__(self, ref, first):
        self.ref, self.first = ref, first

    def __getitem__(self, index):
        rows, columns = index
        return self.ref[pl.ds(rows.start + self.first, rows.size, stride=rows.stride), columns]


def parts(whole):
    return [Rows(whole, first) for first in (0, 640, 1040)]


def pack_kernel(whole, aggregate, packed_out):
    rhs, inverse, coeffs = parts(whole)
    lane = lanes()
    index = slot_columns(lane)
    window = lane >> 3
    sources = {"r": rhs, "j": inverse, "a": coeffs}
    for q in range(PACKED // 8):
        packed = jnp.zeros((8, 128), F32)
        for k, (kind, start) in enumerate(GROUPS[4 * q : 4 * q + 4]):
            for x in range(4):
                if kind == "g":
                    block = jnp.broadcast_to(aggregate[pl.ds(x, 1), :].astype(F32), (8, 128))
                else:
                    block = sources[kind][pl.ds(4 * start + x, 8, stride=4), :]
                packed = jnp.where(window == 4 * k + x, pick(block, index), packed)
        packed_out[pl.ds(8 * q, 8), :] = packed


def raw_kernel(packed, whole, aggregate, raw_b, raw_a):
    rhs, inverse, coeffs = parts(whole)
    odd = odd_tile()
    raw_message(raw_b, odd, rhs, inverse, coeffs, aggregate)
    raw_message(raw_a, 1 - odd, rhs, inverse, coeffs, aggregate)


def merge_kernel(got_1, got_2, mine):
    lane = lanes()
    slot = lane & 7
    odd = lax.rem(lax.axis_index("sub"), 2) == 1
    for q in range(PACKED // 8):
        one, two = got_1[pl.ds(8 * q, 8), :], got_2[pl.ds(8 * q, 8), :]
        left, right = jnp.where(odd, one, two), jnp.where(odd, two, one)
        mine[pl.ds(8 * q, 8), :] = jnp.where(slot <= 2, right, jnp.where(slot >= 5, left, 0.0))


def block_rows(coeff_row, vectors):
    out = []
    for i in range(10):
        pair = None
        for j in range(10):
            m = coeff_row(i, j)
            if pair is None:
                pair = [m * vectors[2 * j], m * vectors[2 * j + 1]]
            else:
                pair = [pair[0] + m * vectors[2 * j], pair[1] + m * vectors[2 * j + 1]]
        out += pair
    return out


def load_slab(ref, base):
    return [ref[pl.ds(base + 8 * b, 8), :] for b in range(20)]


def store_slab(ref, base, values):
    for b in range(20):
        ref[pl.ds(base + 8 * b, 8), :] = values[b]


def at_slab(x):
    return x * FC if isinstance(x, int) else pl.multiple_of(x * FC, 8)


def inverse_at(inverse, x, vectors):
    base = x * IJ if isinstance(x, int) else pl.multiple_of(x * IJ, 8)
    return block_rows(lambda i, j: row(inverse, base + (10 * i + j)), vectors)


def neighbour(source, x, n):
    base = at_slab(x)
    if isinstance(x, int) and x == STRIP:
        shift = (0, 8, -8, -1, 1)[n]
        return [roll(v, shift) for v in load_slab(source, base)]
    if n < 3:
        return load_slab(source, base + (0, -FC, FC)[n])
    lane = lanes()
    out = []
    for b in range(20):
        value = source[pl.ds(base + 8 * b, 8), :]
        strip = source[pl.ds(STRIP * FC + 8 * b, 8), :]
        if n == 3:
            out.append(jnp.where(lane == 0, pltpu.roll(strip, 123 - 8 * x, 1), roll(value, 1)))
        else:
            out.append(jnp.where(lane == 127, pltpu.roll(strip, 125 - 8 * x, 1), roll(value, -1)))
    return out


def stencil_at(coeffs, source, x, moved):
    total = None
    if isinstance(x, int):
        base = 8 * NIJ
    else:
        base = pl.multiple_of((x - 1) * NIJ, 8)
    through = range(1, 5) if isinstance(x, int) else range(3, 5)
    for n in through:
        store_slab(moved, (n - 1) * FC, neighbour(source, x, n))
    for n in range(5):
        vectors = load_slab(moved, (n - 1) * FC) if n in through else neighbour(source, x, n)
        part = block_rows(lambda i, j: row(coeffs, base + (100 * n + 10 * i + j)), vectors)
        total = part if total is None else [a + b for a, b in zip(total, part)]
    return total


def copy_columns(ref, x, values):
    lane = lanes()
    own = (lane == 8 * x + 3) | (lane == 8 * x + 4)
    for b in range(20):
        at = pl.ds(STRIP * FC + 8 * b, 8)
        ref[at, :] = jnp.where(own, pltpu.roll(values[b], 8 * x + 4, 1), ref[at, :])


def over(low, high, step):
    step(STRIP)

    def at(x, carry):
        step(x)
        return carry

    lax.fori_loop(low, high + 1, at, 0)


def down_kernel(
    whole, aggregate, mine, raw_b, raw_a, strip_a, strip_b,
    coeffs_x, inverse_x, smoothed, residual, index_s, index_t, out,
    rhs_x, first, scaled, filtered, moved,
):
    lane = lanes()
    slot = lane & 7
    rhs, inverse, coeffs = parts(whole)
    odd = odd_tile() == 1
    needed = (lane >= 8) & (lane < 72) & ((slot == 1) | (slot == 2) | (slot == 5) | (slot == 6))
    for q in range(PACKED // 8):
        at = pl.ds(8 * q, 8)
        a, b, own = strip_a[at, :], strip_b[at, :], mine[at, :]
        before, after = jnp.where(odd, a, b), jnp.where(odd, b, a)
        for k, (kind, start) in enumerate(GROUPS[4 * q : 4 * q + 4]):
            placed = jnp.where(
                lane < 24,
                roll(before, -32 * k - 8),
                jnp.where(lane < 56, roll(own, 24 - 32 * k), roll(after, 56 - 32 * k)),
            )
            if kind == "r":
                rhs_x[pl.ds(STRIP * FC + start, 8), :] = jnp.where(lane < 80, placed, 0.0)
            elif kind == "j":
                inverse_x[pl.ds(STRIP * IJ + start, 8), :] = jnp.where(lane < 80, placed, 0.0)
            elif kind == "a":
                coeffs_x[pl.ds(8 * NIJ + start, 8), :] = jnp.where(needed, placed, 0.0)
            else:
                index_s[...] = jnp.where(lane < 80, placed, 0.0)
    for x in range(4):
        for kind, start in GROUPS:
            at = pl.ds(4 * start + x, 8, stride=4)
            if kind == "r":
                rhs_x[pl.ds((x + 3) * FC + start, 8), :] = rhs[at, :]
            elif kind == "j":
                inverse_x[pl.ds((x + 3) * IJ + start, 8), :] = inverse[at, :]
            elif kind == "a":
                coeffs_x[pl.ds((x + 2) * NIJ + start, 8), :] = coeffs[at, :]

    def outer(at_raw, count, ref, at_before, at_after):
        for start in range(0, count, 8):
            a, b = raw_a[pl.ds(at_raw + start, 8), :], raw_b[pl.ds(at_raw + start, 8), :]
            ref[pl.ds(at_before + start, 8), :] = jnp.where(odd, a, b)
            ref[pl.ds(at_after + start, 8), :] = jnp.where(odd, b, a)

    outer(0, 3 * FC, rhs_x, 0, 7 * FC)
    outer(RAW_J, 3 * IJ, inverse_x, 0, 7 * IJ)
    outer(RAW_A, 2 * NIJ, coeffs_x, 0, 6 * NIJ)
    a, b = raw_a[pl.ds(RAW_G, 8), :], raw_b[pl.ds(RAW_G, 8), :]
    sublane = lax.broadcasted_iota(I32, (8, 128), 0)
    after = jnp.where(odd, b, a)
    index_t[...] = jnp.where(sublane < 2, jnp.where(odd, a, b), pltpu.roll(after, 2, 0))

    def start_step(x):
        values = [OMEGA * v for v in inverse_at(inverse_x, x, load_slab(rhs_x, at_slab(x)))]
        if not isinstance(x, int):
            copy_columns(first, x, values)
        store_slab(first, at_slab(x), values)

    over(0, 9, start_step)

    def smooth_step(x):
        base = at_slab(x)
        total = stencil_at(coeffs_x, first, x, moved)
        left = [r - t for r, t in zip(load_slab(rhs_x, base), total)]
        step = inverse_at(inverse_x, x, left)
        values = [v + OMEGA * s for v, s in zip(load_slab(first, base), step)]
        if not isinstance(x, int):
            copy_columns(smoothed, x, values)
        store_slab(smoothed, base, values)

    over(1, 8, smooth_step)

    def residual_step(x):
        base = at_slab(x)
        total = stencil_at(coeffs_x, smoothed, x, moved)
        store_slab(residual, base, [r - t for r, t in zip(load_slab(rhs_x, base), total)])
        store_slab(scaled, base, inverse_at(inverse_x, x, load_slab(residual, base)))

    over(2, 7, residual_step)

    def filter_step(x, carry):
        base = at_slab(x)
        total = stencil_at(coeffs_x, scaled, x, moved)
        store_slab(filtered, at_slab(x - 3), [r - THETA * t for r, t in zip(load_slab(residual, base), total)])
        return carry

    lax.fori_loop(3, 7, filter_step, 0)
    member = lax.broadcasted_iota(I32, (128, 128), 0) & 63
    summed = jnp.zeros((FC, 128), F32)
    for x in range(4):
        owner = jnp.broadcast_to(aggregate[pl.ds(x, 1), :], (128, 128))
        table = (owner == member).astype(F32).astype(jnp.bfloat16)
        rest = filtered[pl.ds(x * FC, FC), :]
        for _ in range(3):
            part = rest.astype(jnp.bfloat16)
            rest = rest - part.astype(F32)
            summed = summed + lax.dot_general(
                part, table, (((1,), (1,)), ((), ())), preferred_element_type=F32
            )
    low = lax.broadcasted_iota(I32, (80, 128), 1) < 64
    packed = jnp.where(low, summed[:80], summed[80:])
    for s in range(4):
        out[s] = packed


def live_lane(index):
    lane = jnp.where(index < 96, index, jnp.where(index < 192, index - 32, index - 80))
    return jnp.where(index >= 256, index - 128, lane)


def live(low, high, lane):
    return jnp.where(lane < 96, low, jnp.where(lane < 112, roll(high, 96), roll(high, 48)))


def send_coarse(index, level, out_a, out_b):
    lane = lanes()
    odd = odd_tile() == 1
    tables = []
    for d in range(2):
        four = jnp.concatenate([index[pl.ds(d, 1), :]] * 4, axis=1)
        tables.append(jnp.broadcast_to(live_lane(four), (8, 128)))
    for out, table in (
        (out_a, jnp.where(odd, tables[0], tables[1])),
        (out_b, jnp.where(odd, tables[1], tables[0])),
    ):
        for g in range(5):
            packed = jnp.zeros((8, 128), F32)
            for k in range(4):
                value = pick(level[pl.ds(8 * (4 * g + k), 8), :], table)
                packed = jnp.where((lane >> 5) == k, value, packed)
            out[pl.ds(8 * g, 8), :] = packed


def coarse_start_kernel(got, coeffs, inverse, send, rhs, level, coeffs_l, inverse_l, out_a, out_b):
    lane = lanes()
    for b in range(20):
        r = 8 * (b % 10)
        up = 64 * (b // 10)
        part = [got[s, pl.ds(r, 8), :] for s in range(4)]
        value = jnp.where(lane < 64, roll(part[0], -up), roll(part[1], 64 - up))
        value = jnp.where(lane < 96, value, jnp.where(lane < 112, roll(part[2], 96 - up), roll(part[3], 112 - up)))
        rhs[pl.ds(8 * b, 8), :] = value
    lane10 = lax.broadcasted_iota(I32, (10, 128), 1)
    for i in range(10):
        inverse_l[i] = live(inverse[i, :, 0:128], inverse[i, :, 128:256], lane10)
    for n in range(5):
        for i in range(10):
            coeffs_l[n, i] = live(coeffs[n, i, :, 0:128], coeffs[n, i, :, 128:256], lane10)
    values = block_rows(lambda i, j: jnp.broadcast_to(inverse_l[i, pl.ds(j, 1), :], (8, 128)), load_slab(rhs, 0))
    store_slab(level, 0, [OMEGA * v for v in values])
    send_coarse(send, level, out_a, out_b)


def sweep(coeffs_l, inverse_l, cols, rhs, level, got_a, got_b):
    lane = lanes()
    odd = odd_tile() == 1
    extra = []
    for g in range(5):
        a, b = got_a[pl.ds(8 * g, 8), :], got_b[pl.ds(8 * g, 8), :]
        before, after = jnp.where(odd, a, b), jnp.where(odd, b, a)
        for k in range(4):
            extra.append(jnp.where(lane < 32, roll(before, -32 * k), roll(after, 32 - 32 * k)))
    total = block_rows(lambda i, j: jnp.broadcast_to(coeffs_l[0, i, pl.ds(j, 1), :], (8, 128)), load_slab(level, 0))
    for n in range(1, 5):
        low, high = cols[pl.ds(n, 1), 0:128], cols[pl.ds(n, 1), 128:256]
        lane1 = lax.broadcasted_iota(I32, (8, 128), 1)
        index = live(jnp.broadcast_to(low, (8, 128)), jnp.broadcast_to(high, (8, 128)), lane1)
        index = live_lane(index)
        near = index & 127
        vectors = []
        for b in range(20):
            own = pick(level[pl.ds(8 * b, 8), :], near)
            vectors.append(jnp.where(index < 128, own, pick(extra[b], near)))
        part = block_rows(lambda i, j: jnp.broadcast_to(coeffs_l[n, i, pl.ds(j, 1), :], (8, 128)), vectors)
        total = [a + b for a, b in zip(total, part)]
    left = [r - t for r, t in zip(load_slab(rhs, 0), total)]
    step = block_rows(lambda i, j: jnp.broadcast_to(inverse_l[i, pl.ds(j, 1), :], (8, 128)), left)
    return [v + OMEGA * s for v, s in zip(load_slab(level, 0), step)]


def sweep_kernel(coeffs_l, inverse_l, cols, send, rhs, level, got_b, got_a, out, out_b, out_a):
    store_slab(out, 0, sweep(coeffs_l, inverse_l, cols, rhs, level, got_a, got_b))
    send_coarse(send, out, out_a, out_b)


def last_sweep_kernel(coeffs_l, inverse_l, cols, rhs, level, got_b, got_a, out):
    store_slab(out, 0, sweep(coeffs_l, inverse_l, cols, rhs, level, got_a, got_b))


def up_kernel(
    coeffs_x, inverse_x, smoothed, residual, aggregate, index_s, index_t, level, got_a, got_b,
    out, spread, applied, scaled, moved,
):
    lane = lanes()
    slot = lane & 7
    odd = odd_tile() == 1
    sub, subs = lax.axis_index("sub"), lax.axis_size("sub")

    def offset(s):
        return jnp.where(s <= 0, 0, jnp.where(s == 1, 64, jnp.where(s == 2, 96, 112)))

    own_at = offset(sub)
    mains = [jnp.minimum(row(aggregate, x) + own_at, 127) for x in range(4)]
    outers = [jnp.minimum(spread_row(index_t, r).astype(I32) + own_at, 127) for r in range(4)]
    side = jnp.where(slot <= 2, offset(sub + 1), offset(sub - 1))
    beside = jnp.minimum(index_s[...].astype(I32) + side, 127)
    there = ((slot <= 2) & (sub < subs - 1)) | ((slot >= 5) & (sub > 0))
    for b in range(20):
        at = pl.ds(8 * b, 8)
        own, va, vb = level[at, :], got_a[at, :], got_b[at, :]
        before, after = jnp.where(odd, va, vb), jnp.where(odd, vb, va)
        strip = jnp.where(
            lane < 24, pick(before, beside), jnp.where(lane < 56, pick(own, beside), pick(after, beside))
        )
        strip = jnp.where(there & (lane < 80), strip, 0.0)
        for x in range(1, 9):
            if x < 3:
                value = pick(before, outers[x - 1])
            elif x < 7:
                value = pick(own, mains[x - 3])
            else:
                value = pick(after, outers[x - 5])
            spread[pl.ds(x * FC + 8 * b, 8), :] = value
            strip = jnp.where((lane == 8 * x + 3) | (lane == 8 * x + 4), roll(value, 8 * x + 4), strip)
        spread[pl.ds(STRIP * FC + 8 * b, 8), :] = strip

    def spread_step(x):
        base = at_slab(x)
        store_slab(applied, base, stencil_at(coeffs_x, spread, x, moved))
        store_slab(scaled, base, inverse_at(inverse_x, x, load_slab(applied, base)))

    over(2, 7, spread_step)

    def last_step(x, carry):
        base = at_slab(x)
        total = stencil_at(coeffs_x, scaled, x, moved)
        left = [
            r - a + THETA * t
            for r, a, t in zip(load_slab(residual, base), load_slab(applied, base), total)
        ]
        step = inverse_at(inverse_x, x, left)
        for b in range(20):
            at = pl.ds(base + 8 * b, 8)
            value = smoothed[at, :] + spread[at, :] - THETA * scaled[at, :] + OMEGA * step[b]
            out[pl.ds(32 * b + x - 3, 8, stride=4), :] = value
        return carry

    lax.fori_loop(3, 7, last_step, 0)


def body(right_side, fine_coeffs, fine_inverse, aggregate, coarse_coeffs, coarse_inverse, coarse_cols, send_rows):
    tiles, subs = lax.axis_size("tile"), lax.axis_size("sub")

    def swaps(count):
        both = []
        for begin in (0, 1):
            pairs = [(i, i + 1) for i in range(begin, count - 1, 2)]
            both.append(pairs + [(b, a) for a, b in pairs])
        return both

    tile_a, tile_b = swaps(tiles)
    sub_1, sub_2 = swaps(subs)

    def trade(to_b, to_a):
        return lax.ppermute(to_b, "tile", tile_b), lax.ppermute(to_a, "tile", tile_a)

    rhs = right_side.reshape(640, 128)
    inverse = fine_inverse.reshape(400, 128)
    coeffs = fine_coeffs.reshape(2000, 128)
    slabs, small, cvec = (SLABS * FC, 128), (40, 128), (FC, 128)

    whole = jnp.concatenate([rhs, inverse, coeffs], axis=0)
    (packed,) = call(pack_kernel, [(PACKED, 128)], [whole, aggregate])
    got_1 = lax.ppermute(packed, "sub", sub_1)
    got_2 = lax.ppermute(packed, "sub", sub_2)
    raw_b, raw_a = call(raw_kernel, [(RAW, 128), (RAW, 128)], [packed, whole, aggregate])
    raw = trade(raw_b, raw_a)
    (mine,) = call(merge_kernel, [(PACKED, 128)], [got_1, got_2])
    strips = trade(mine, mine)[::-1]
    coeffs_x, inverse_x, smoothed, residual, index_s, index_t, summed = call(
        down_kernel,
        [(9 * NIJ, 128), (SLABS * IJ, 128), slabs, slabs, (8, 128), (8, 128), (4, 80, 128)],
        [whole, aggregate, mine, *raw, *strips],
        [slabs, slabs, slabs, (4 * FC, 128), (4 * FC, 128)],
    )
    summed = lax.all_to_all(summed, "sub", 0, 0)
    group_rhs, level, coeffs_l, inverse_l, out_a, out_b = call(
        coarse_start_kernel,
        [cvec, cvec, (5, 10, 10, 128), (10, 10, 128), small, small],
        [summed, coarse_coeffs, coarse_inverse, send_rows],
    )
    for _ in range(CSWEEP - 2):
        level, out_b, out_a = call(
            sweep_kernel,
            [cvec, small, small],
            [coeffs_l, inverse_l, coarse_cols, send_rows, group_rhs, level, *trade(out_b, out_a)],
        )
    (level,) = call(
        last_sweep_kernel,
        [cvec],
        [coeffs_l, inverse_l, coarse_cols, group_rhs, level, *trade(out_b, out_a)],
    )
    (out,) = call(
        up_kernel,
        [(640, 128)],
        [coeffs_x, inverse_x, smoothed, residual, aggregate, index_s, index_t, level, *trade(level, level)[::-1]],
        [slabs, slabs, slabs, (4 * FC, 128)],
    )
    return out.reshape(right_side.shape)


def solution(mesh):
    in_specs = (
        P(None, None, "tile", "sub"),
        P(None, None, None, "tile", "sub"),
        P(None, None, "tile", "sub"),
        P("tile", "sub"),
        P(None, None, None, "tile"),
        P(None, None, "tile"),
        P(None, "tile"),
        P(None, "tile"),
    )
    out_specs = P(None, None, "tile", "sub")
    return jax.shard_map(body, mesh=mesh, in_specs=in_specs, out_specs=out_specs, check_vma=False)
```
